32 devices in a mesh: shard: 4 (over z), ctx: 4 (over y, x), tp: 2 (over core).
Axes of the slice: x: 2, y: 2, z: 4, core: 2. Of those that a mesh axis runs over, the one named last changes fastest.
Arguments:
- tokens: bfloat16 [8192, 2048], P(('shard', 'ctx')), may hold values from -6 to 6
- cotangent: bfloat16 [8192, 2048], P(('shard', 'ctx')), may hold values from -6 to 6
- lengths: int32 [4, 3], P('shard'), may hold values from 1 to 320, 512 in all within a row
- norm_gain: float32 [2, 2, 2048], replicated, may hold values from 0.5 to 1.5
- norm_bias: float32 [2, 2, 2048], replicated, may hold values from -1.75 to 1.75
- input_bias: float32 [2, 3, 2048], P(None, None, 'tp'), may hold values from -1.75 to 1.75
- input_projection: bfloat16 [2, 2048, 3, 2048], P(None, ('shard', 'ctx'), None, 'tp'), may hold values from -0.125 to 0.125
- output_projection: bfloat16 [2, 2048, 2048], P(None, ('shard', 'ctx'), 'tp'), may hold values from -0.5 to 0.5
- gate_up_weight: bfloat16 [2, 2048, 2, 5632], P(None, ('shard', 'ctx'), None, 'tp'), may hold values from -0.125 to 0.125
- down_weight: bfloat16 [2, 2048, 5632], P(None, ('shard', 'ctx'), 'tp'), may hold values from -0.078125 to 0.078125
Outputs:
- result: bfloat16 [8192, 2048], P(('shard', 'ctx'))
- tokens_grad: float32 [8192, 2048], P(('shard', 'ctx'))
- norm_gain_grad: float32 [2, 2, 2048], replicated
- norm_bias_grad: float32 [2, 2, 2048], replicated
- input_bias_grad: float32 [2, 3, 2048], P(None, None, 'tp')
- input_projection_grad: float32 [2, 2048, 3, 2048], P(None, ('shard', 'ctx'), None, 'tp')
- output_projection_grad: float32 [2, 2048, 2048], P(None, ('shard', 'ctx'), 'tp')
- gate_up_grad: float32 [2, 2048, 2, 5632], P(None, ('shard', 'ctx'), None, 'tp')
- down_grad: float32 [2, 2048, 5632], P(None, ('shard', 'ctx'), 'tp')
The draws below stay inside these ranges and needn't reach their ends.
Inputs may be any that keep to these rules, and one draw needn't show every extreme that they name: `lengths`: row s gives, for the 3 sequences of shard index s, the tokens of each on one device of ctx: a sequence has 4 times as many tokens, cut into equal consecutive pieces in ctx order, and every device stores its pieces in the order of the sequences. Each row sums to 512; the largest entry of each row is exactly 320.
All inputs are finite; a program needn't handle non-finite values.
Results may differ from the reference program's by a relative error of at most 0.019.
Values may be sent and summed in bfloat16 or wider, within the bound.
No kernel may reach another device: no remote copies, remote signals or barrier semaphores. Data moves between devices by JAX's collectives and lax.ppermute only.
A program may use at most 448 MiB of HBM per device.

```python
import math
import jax
import jax.numpy as jnp
import numpy as np
from jax import lax

D = 2048
HEADS = 32
HEAD = 64
ROT = 16
FF = 5632
LAYERS = 2
NSEQ = 3
TOK_DEV = 512
MOST = 320
TOKENS = 8192
N_SHARD = 4
N_CTX = 4


def block_levels(stream_key, extent, shards, least, largest):
    level = 1.0
    for axis_at, blocks in shards:
        steps = jax.random.uniform(jax.random.fold_in(jax.random.fold_in(stream_key, 6), axis_at), (blocks,), jnp.float32, least / len(shards), largest / len(shards))
        level = level * jnp.repeat(jnp.exp(steps), extent[axis_at] // blocks).reshape((-1,) + (1,) * (len(extent) - 1 - axis_at))
    return level


def split_up(amount, total, most, lean):
    loads = [(1 << 20) // math.isqrt(grade ** lean) + 1 for grade in range(2, amount + 1)]
    spare, counts = total - most - (amount - 1), [1] * (amount - 1)
    while spare > 0:
        movable = [i for i in range(amount - 1) if counts[i] < most]
        pool, remaining = sum([loads[i] for i in movable]), spare
        for i in movable:
            addition = min(most - counts[i], max(1, remaining * loads[i] // pool), spare)
            counts[i] = counts[i] + addition
            spare = spare - addition
    return np.array([most] + counts)


def ragged(rng, count, total, reach, slope):
    if count == 2:
        one = jax.random.randint(rng, (), max(1, total - reach), min(reach, total - 1) + 1)
        return jnp.stack([one, total - one])
    sizes = jnp.asarray(split_up(count, total, reach, slope), jnp.int32)
    pairs = (count - 1) // 2
    giver, receiver = sizes[1:1 + 2 * pairs:2], sizes[2:2 + 2 * pairs:2]
    room = jnp.minimum(giver - 1, reach - receiver)
    passed = jax.random.randint(jax.random.fold_in(rng, 1), (pairs,), 0, 1 << 20) % (room + 1)
    sizes = sizes.at[1:1 + 2 * pairs:2].set(giver - passed).at[2:2 + 2 * pairs:2].set(receiver + passed)
    return sizes[jax.random.permutation(jax.random.fold_in(rng, 2), count)]


def noise(own_key, extent, deviation, most, shards=(), kind=jnp.bfloat16):
    result = deviation * jax.random.normal(own_key, extent, jnp.float32)
    if shards:
        result = result * block_levels(own_key, extent, shards, -0.22, 0.18)
    return jnp.clip(result, -most, most).astype(kind)


def setup_inputs(seed: int = 0) -> dict:
    seeds = jax.random.split(jax.random.key(seed), 11)
    return {
        "tokens": noise(seeds[0], (TOKENS, D), 1.0, 6.0, ((0, 16),)),
        "cotangent": noise(seeds[1], (TOKENS, D), 1.0, 6.0, ((0, 16),)),
        "lengths": jax.vmap(lambda own: ragged(own, NSEQ, TOK_DEV, MOST, 1))(jax.random.split(seeds[2], N_SHARD)).reshape((N_SHARD, NSEQ)).astype(jnp.int32),
        "norm_gain": jnp.clip(1.0 + 0.1 * jax.random.normal(seeds[3], (LAYERS, 2, D), jnp.float32), 0.5, 1.5),
        "norm_bias": noise(seeds[4], (LAYERS, 2, D), 0.3, 1.75, (), jnp.float32),
        "input_bias": noise(seeds[5], (LAYERS, 3, D), 0.3, 1.75, ((2, 2),), jnp.float32),
        "input_projection": noise(seeds[6], (LAYERS, D, 3, D), D ** -0.5, 0.125, ((1, 16), (3, 2))),
        "output_projection": noise(seeds[7], (LAYERS, D, D), (D // 16) ** -0.5, 0.5, ((1, 16), (2, 2))),
        "gate_up_weight": noise(seeds[8], (LAYERS, D, 2, FF), D ** -0.5, 0.125, ((1, 16), (3, 2))),
        "down_weight": noise(seeds[9], (LAYERS, D, FF), FF ** -0.5, 0.078125, ((1, 16), (2, 2))),
    }


@jax.custom_vjp
def low(v):
    return lax.optimization_barrier(v.astype(jnp.bfloat16)).astype(jnp.float32)

@jax.custom_vjp
def low_back(v):
    return v

def low_keep(v):
    return (low(v), None)

def low_pass(kept, grad):
    return (grad,)

def back_keep(v):
    return (v, None)

def back_low(kept, grad):
    return (low(grad),)
low.defvjp(low_keep, low_pass)
low_back.defvjp(back_keep, back_low)
highest = lax.Precision.HIGHEST
norm_eps = 1e-05
rotary_base = 10000.0

def row_meta(seq_lengths, row_count):
    seq_ends = jnp.cumsum(seq_lengths, dtype=jnp.int32)
    row_index = jnp.arange(row_count, dtype=jnp.int32)
    seq_ids = lax.optimization_barrier(jnp.sum((row_index[:, None] >= seq_ends[None, :]).astype(jnp.int32), axis=1, dtype=jnp.int32))
    one_hot = (seq_ids[:, None] == jnp.arange(seq_lengths.shape[0], dtype=jnp.int32)[None, :]).astype(jnp.int32)
    seq_start = lax.optimization_barrier(jnp.sum(one_hot * (seq_ends - seq_lengths)[None, :], axis=1, dtype=jnp.int32))
    length = lax.optimization_barrier(jnp.sum(one_hot * seq_lengths[None, :], axis=1, dtype=jnp.int32))
    return (seq_ids, length, row_index - seq_start)

def group_meta(seq_lengths):
    seq_ids, length, offset = row_meta(seq_lengths, TOK_DEV)
    devices = jnp.arange(N_CTX, dtype=jnp.int32)[:, None]
    return (jnp.tile(seq_ids, N_CTX), (devices * length[None, :] + offset[None, :]).reshape(-1))

def rotary_tables(positions):
    half_rot = ROT // 2
    frequency = rotary_base ** (-(2.0 * jnp.arange(half_rot, dtype=jnp.float32)) / ROT)
    angles = positions.astype(jnp.float32)[:, None] * frequency[None, :]
    return (jnp.cos(angles), jnp.sin(angles))

def rotate(vectors, cosine, sine):
    half_rot = cosine.shape[-1]
    lead_half = vectors[..., :half_rot]
    trail_half = vectors[..., half_rot:2 * half_rot]
    cos_wide = cosine[:, None, :]
    sin_wide = sine[:, None, :]
    return jnp.concatenate([lead_half * cos_wide - trail_half * sin_wide, trail_half * cos_wide + lead_half * sin_wide, vectors[..., 2 * half_rot:]], axis=-1)

def layer_norm(stream, gain_row, bias_row):
    row_mean = lax.optimization_barrier(jnp.mean(stream, axis=-1, keepdims=True))
    centered = stream - row_mean
    variance = lax.optimization_barrier(jnp.mean(centered * centered, axis=-1, keepdims=True))
    return centered * lax.rsqrt(variance + norm_eps) * gain_row + bias_row

def attention_group(operands):
    queries, keys_all, values_all, seq_ids, positions = operands
    allowed = (seq_ids[:, None] == seq_ids[None, :]) & (positions[None, :] <= positions[:, None])
    score_scale = float(HEAD) ** (-0.5)

    def one_head(head_operands):
        query_head, key_head, value_head = head_operands
        scores = low_back(jnp.dot(query_head, key_head.T, precision=highest) * score_scale)
        scores = jnp.where(allowed, scores, -1e+30)
        probs = jax.nn.softmax(scores, axis=-1)
        return jnp.dot(low(probs), value_head, precision=highest)
    outputs = lax.map(jax.checkpoint(one_head), (queries.transpose(1, 0, 2), keys_all.transpose(1, 0, 2), values_all.transpose(1, 0, 2)))
    return outputs.transpose(1, 0, 2)

def forward(stream, norm_gain, norm_bias, input_bias, input_projection, output_projection, gate_up_weight, down_weight, seq_ids, positions, cosine, sine):
    token_count = stream.shape[0]
    group_rows = TOK_DEV * N_CTX

    def grouped(tensor):
        return tensor.reshape(N_SHARD, group_rows, HEADS, HEAD)
    for layer_index in range(LAYERS):
        normed = low(layer_norm(stream, norm_gain[layer_index, 0], norm_bias[layer_index, 0]))
        joined = jnp.einsum('td,dch->tch', normed, input_projection[layer_index], precision=highest) + input_bias[layer_index]
        joined = low_back(joined).reshape(token_count, 3, HEADS, HEAD)
        queries = low(rotate(joined[:, 0], cosine, sine))
        keys_all = low(rotate(joined[:, 1], cosine, sine))
        values_all = low(joined[:, 2])
        outputs = lax.map(attention_group, (grouped(queries), grouped(keys_all), grouped(values_all), seq_ids, positions))
        outputs = low(low_back(outputs.reshape(token_count, D)))
        stream = stream + low_back(jnp.einsum('th,dh->td', outputs, output_projection[layer_index], precision=highest))
        normed = low(layer_norm(stream, norm_gain[layer_index, 1], norm_bias[layer_index, 1]))
        gate_up = low_back(jnp.einsum('td,dcf->tcf', normed, gate_up_weight[layer_index], precision=highest))
        hidden = low(jax.nn.silu(gate_up[:, 0]) * gate_up[:, 1])
        stream = stream + low_back(jnp.einsum('tf,df->td', hidden, down_weight[layer_index], precision=highest))
    return stream

def reference(tokens, cotangent, lengths, norm_gain, norm_bias, input_bias, input_projection, output_projection, gate_up_weight, down_weight):
    seq_ids, positions = jax.vmap(group_meta)(lengths)
    cosine, sine = rotary_tables(positions.reshape(-1))

    def run(*params):
        return forward(*params, seq_ids, positions, cosine, sine)
    floats = (tokens.astype(jnp.float32), norm_gain.astype(jnp.float32), norm_bias.astype(jnp.float32), input_bias.astype(jnp.float32), input_projection.astype(jnp.float32), output_projection.astype(jnp.float32), gate_up_weight.astype(jnp.float32), down_weight.astype(jnp.float32))
    output, pullback = jax.vjp(run, *floats)
    grads = pullback(cotangent.astype(jnp.float32))
    return (output.astype(jnp.bfloat16), grads[0], grads[1], grads[2], grads[3], grads[4], grads[5], grads[6], grads[7])
```

```python
import functools
import math

import jax
import jax.numpy as jnp
from jax import lax
from jax.experimental import pallas as pl
from jax.experimental.pallas import tpu as pltpu
from jax.sharding import PartitionSpec as P

HEAD = 64
ROT = 16
LANES = 128

norm_eps = 1e-05
rotary_base = 10000.0
blocked = -(2.0**100)
low = jnp.bfloat16
full = jnp.float32


def row_meta(seq_lengths, row_count):
    seq_ends = jnp.cumsum(seq_lengths, dtype=jnp.int32)
    row_index = jnp.arange(row_count, dtype=jnp.int32)
    seq_ids = jnp.sum(
        (row_index[:, None] >= seq_ends[None, :]).astype(jnp.int32), axis=1, dtype=jnp.int32
    )
    one_hot = (
        seq_ids[:, None] == jnp.arange(seq_lengths.shape[0], dtype=jnp.int32)[None, :]
    ).astype(jnp.int32)
    seq_start = jnp.sum(one_hot * (seq_ends - seq_lengths)[None, :], axis=1, dtype=jnp.int32)
    length = jnp.sum(one_hot * seq_lengths[None, :], axis=1, dtype=jnp.int32)
    return (seq_ids, length, row_index - seq_start)


def wide_rotary_tables(positions):
    half_rot = ROT // 2
    frequency = rotary_base ** (-(2.0 * jnp.arange(half_rot, dtype=full)) / ROT)
    lane = jnp.arange(LANES, dtype=jnp.int32) % HEAD
    lane_frequency = jnp.where(lane < ROT, jnp.tile(frequency, LANES // half_rot), 0.0)
    sign = jnp.where(lane < half_rot, -1.0, 1.0)
    angles = positions.astype(full)[:, None] * lane_frequency[None, :]
    return (jnp.cos(angles), jnp.sin(angles) * sign[None, :])


def norm_parts(stream, gain_row, bias_row):
    row_mean = jnp.mean(stream, axis=-1, keepdims=True)
    centered = stream - row_mean
    variance = jnp.mean(centered * centered, axis=-1, keepdims=True)
    inverse = lax.rsqrt(variance + norm_eps)
    scaled = centered * inverse
    return (scaled, inverse, scaled * gain_row + bias_row)


def norm_back(grad_normed, scaled, inverse, gain_row):
    grad_scaled = grad_normed * gain_row
    inner = (
        grad_scaled
        - jnp.mean(grad_scaled, axis=-1, keepdims=True)
        - scaled * jnp.mean(grad_scaled * scaled, axis=-1, keepdims=True)
    )
    return (inverse * inner, jnp.sum(grad_normed * scaled, axis=0), jnp.sum(grad_normed, axis=0))


def dot_nn(left, right):
    return lax.dot_general(left, right, (((1,), (0,)), ((), ())), preferred_element_type=full)


def dot_nt(left, right):
    return lax.dot_general(left, right, (((1,), (1,)), ((), ())), preferred_element_type=full)


def dot_tn(left, right):
    return lax.dot_general(left, right, (((0,), (0,)), ((), ())), preferred_element_type=full)


def partner(values, lane):
    near = pltpu.roll(values, LANES - ROT // 2, 1)
    far = pltpu.roll(values, ROT // 2, 1)
    return jnp.where(lane % HEAD < ROT // 2, near, far)


def attend_kernel(ctx_count, tp_count, slots, order_ref, *refs):
    normed_refs = refs[:slots]
    weight_ref, bias_ref, cos_ref, sin_ref, query_mark_ref, key_mark_ref = refs[slots : slots + 6]
    out_refs = refs[slots + 6 : 2 * slots + 6]
    fine_ref, total_ref, rotated_ref, key_wide = refs[2 * slots + 6 :]
    rows_all = rotated_ref.shape[0]
    block = rows_all // ctx_count
    part = block // tp_count
    slot_parts = ctx_count * tp_count // slots
    lane_part = lax.broadcasted_iota(jnp.int32, (part, LANES), 1)
    to_exponent = float(HEAD) ** (-0.5) * math.log2(math.e)

    for place in range(ctx_count * tp_count):
        slot, start = place // slot_parts, place % slot_parts * part
        source = slice(start, start + part)
        target = pl.ds(pl.multiple_of(order_ref[place] * part, part), part)
        mark = pl.ds(pl.multiple_of(lax.rem(order_ref[place], tp_count) * part, part), part)
        cosine = cos_ref[target, :]
        sine = sin_ref[target, :]
        joined = dot_nn(normed_refs[slot][source, :], weight_ref[...])
        for kind in range(3):
            columns = slice(kind * LANES, (kind + 1) * LANES)
            values = joined[:, columns] + bias_ref[0, kind : kind + 1, :]
            if kind < 2:
                values = values * cosine + partner(values, lane_part) * sine
            rotated_ref[target, columns] = values.astype(low)
        key_wide[target, :LANES] = rotated_ref[target, LANES : 2 * LANES]
        key_wide[target, LANES:] = key_mark_ref[mark, :]

    tile = min(256, block)
    lane_tile = lax.broadcasted_iota(jnp.int32, (tile, LANES), 1)
    row_index = lax.broadcasted_iota(jnp.int32, (tile, block), 0)
    column_index = lax.broadcasted_iota(jnp.int32, (tile, block), 1)
    for place in range(ctx_count):
        past = place * block
        for head in range(2):

            def step(sub, unused):
                start = pl.multiple_of(sub * tile, tile)
                rows = pl.ds(pl.multiple_of(past + sub * tile, tile), tile)
                own_lanes = lane_tile // HEAD == head
                query = rotated_ref[rows, :LANES]
                query = jnp.concatenate(
                    [
                        jnp.where(own_lanes, query, jnp.zeros_like(query)),
                        query_mark_ref[pl.ds(start, tile), :],
                    ],
                    axis=1,
                )
                near = dot_nt(query, key_wide[past : past + block, :])
                near = jnp.where(column_index <= row_index + start, near, blocked)
                top = jnp.max(near, axis=1, keepdims=True)
                if past:
                    far = dot_nt(query, key_wide[:past, :])
                    top = jnp.maximum(top, jnp.max(far, axis=1, keepdims=True))
                shift = top * to_exponent
                near = jnp.exp2(near * to_exponent - shift)
                total = jnp.sum(near, axis=1, keepdims=True)
                out = dot_nn(near.astype(low), rotated_ref[past : past + block, 2 * LANES :])
                if past:
                    far = jnp.exp2(far * to_exponent - shift)
                    total = total + jnp.sum(far, axis=1, keepdims=True)
                    out = out + dot_nn(far.astype(low), rotated_ref[:past, 2 * LANES :])
                out = out / total
                fine_ref[rows, :] = jnp.where(own_lanes, out, fine_ref[rows, :])
                log_total = jnp.broadcast_to(shift + jnp.log2(total), (tile, LANES))
                total_ref[0, head : head + 1, rows] = jnp.transpose(log_total)[:1, :]
                return unused

            lax.fori_loop(0, block // tile, step, 0)

    for place in range(ctx_count * tp_count):
        slot, start = place // slot_parts, place % slot_parts * part
        source = pl.ds(pl.multiple_of(order_ref[place] * part, part), part)
        out_refs[slot][start : start + part, :] = fine_ref[source, :].astype(low)


def attend_back_kernel(ctx_count, tp_count, slots, order_ref, rotated_ref, *refs):
    grad_refs = refs[:slots]
    fine_ref, total_ref, cos_ref, sin_ref, query_mark_ref, key_mark_ref = refs[slots : slots + 6]
    out_refs = refs[slots + 6 : 2 * slots + 6]
    (
        sum_ref,
        query_wide,
        key_wide,
        key_turned,
        grad_own,
        row_dots,
        grad_query,
        grad_key,
        grad_value,
        query_rows_grad,
    ) = refs[2 * slots + 6 :]
    rows_all = rotated_ref.shape[0]
    slot_parts = ctx_count * tp_count // slots
    block = rows_all // ctx_count
    part = block // tp_count
    score_scale = float(HEAD) ** (-0.5)
    to_exponent = score_scale * math.log2(math.e)
    lane_block = lax.broadcasted_iota(jnp.int32, (block, LANES), 1)
    lane_part = lax.broadcasted_iota(jnp.int32, (part, LANES), 1)
    head_row = lax.broadcasted_iota(jnp.int32, (LANES, block), 0)

    for place in range(ctx_count * tp_count):
        slot, start = place // slot_parts, place % slot_parts * part
        target = pl.ds(pl.multiple_of(order_ref[place] * part, part), part)
        grad_own[0, target, :] = grad_refs[slot][start : start + part, :]

    def prepare(place, unused):
        rows = pl.ds(pl.multiple_of(place * block, block), block)
        grad = grad_own[0, rows, :]
        product = jnp.transpose(grad.astype(full) * fine_ref[rows, :])
        turned = jnp.transpose(rotated_ref[rows, LANES : 2 * LANES].astype(full))
        query = rotated_ref[rows, :LANES]
        for head in range(2):
            own_lanes = lane_block // HEAD == head
            row_dots[head : head + 1, rows] = jnp.sum(
                product[head * HEAD : (head + 1) * HEAD, :], axis=0, keepdims=True
            )
            key_turned[head, :, rows] = jnp.where(head_row // HEAD == head, turned, 0.0).astype(low)
            query_wide[head, rows, :LANES] = jnp.where(own_lanes, query, jnp.zeros_like(query))
            query_wide[head, rows, LANES:] = query_mark_ref[...]
            grad_own[head, rows, :] = jnp.where(own_lanes, grad, jnp.zeros_like(grad))
        key_wide[rows, :LANES] = rotated_ref[rows, LANES : 2 * LANES]
        key_wide[rows, LANES:] = key_mark_ref[...]
        grad_query[:, rows] = jnp.zeros((LANES, block), full)
        grad_key[rows, :] = jnp.zeros((block, LANES), full)
        grad_value[rows, :] = jnp.zeros((block, LANES), full)
        return unused

    lax.fori_loop(0, ctx_count, prepare, 0)

    key_index = lax.broadcasted_iota(jnp.int32, (block, block), 0)
    query_index = lax.broadcasted_iota(jnp.int32, (block, block), 1)

    def pair(head, key_rows, query_rows, diagonal):
        query = query_wide[head, query_rows, :]
        scores = dot_nt(key_wide[key_rows, :], query)
        if diagonal:
            scores = jnp.where(key_index <= query_index, scores, blocked)
        probs = jnp.exp2(scores * to_exponent - total_ref[0, head : head + 1, query_rows])
        grad = grad_own[head, query_rows, :]
        grad_probs = dot_nt(rotated_ref[key_rows, 2 * LANES :], grad)
        grad_scores = (probs * (grad_probs - row_dots[head : head + 1, query_rows])).astype(low)
        grad_value[key_rows, :] += dot_nn(probs.astype(low), grad)
        grad_key[key_rows, :] += dot_nn(grad_scores, query[:, :LANES])
        grad_query[:, query_rows] += dot_nn(key_turned[head, :, key_rows], grad_scores)

    for head in range(2):

        def over_keys(key_place, unused, head=head):
            key_rows = pl.ds(pl.multiple_of(key_place * block, block), block)
            pair(head, key_rows, key_rows, True)

            def over_queries(query_place, inner):
                pair(head, key_rows, pl.ds(pl.multiple_of(query_place * block, block), block), False)
                return inner

            return lax.fori_loop(key_place + 1, ctx_count, over_queries, unused)

        lax.fori_loop(0, ctx_count, over_keys, 0)

    sum_ref[...] = jnp.zeros_like(sum_ref)

    def turn(place, unused):
        rows = pl.ds(pl.multiple_of(place * block, block), block)
        query_rows_grad[rows, :] = jnp.transpose(grad_query[:, rows])
        return unused

    lax.fori_loop(0, ctx_count, turn, 0)

    for place in range(ctx_count * tp_count):
        slot, start = place // slot_parts, place % slot_parts * part
        source = pl.ds(pl.multiple_of(order_ref[place] * part, part), part)
        cosine = cos_ref[source, :]
        sine = sin_ref[source, :]
        values = (
            query_rows_grad[source, :] * score_scale,
            grad_key[source, :] * score_scale,
            grad_value[source, :],
        )
        for kind in range(3):
            value = values[kind]
            if kind < 2:
                value = value * cosine - partner(value, lane_part) * sine
            value = value.astype(low)
            out_refs[slot][start : start + part, kind * LANES : (kind + 1) * LANES] = value
            sum_ref[0, kind : kind + 1, :] += jnp.sum(value.astype(full), axis=0, keepdims=True)


def whole(shape):
    return pl.BlockSpec(shape, lambda pair: (0,) * len(shape))


def attend(order, normed, weight, bias, tables, ctx_count, tp_count):
    slots = len(normed)
    slot_rows, features = normed[0].shape
    rows = slots * slot_rows
    pairs = bias.shape[0]
    width = pairs * 3 * LANES
    trio = pl.BlockSpec((rows, 3 * LANES), lambda pair: (0, pair))
    single = pl.BlockSpec((rows, LANES), lambda pair: (0, pair))
    slot_single = pl.BlockSpec((slot_rows, LANES), lambda pair: (0, pair))
    results = pl.pallas_call(
        functools.partial(attend_kernel, ctx_count, tp_count, slots),
        grid=(pairs,),
        in_specs=[pl.BlockSpec(memory_space=pltpu.SMEM)]
        + [whole((slot_rows, features))] * slots
        + [pl.BlockSpec((features, 3 * LANES), lambda pair: (0, pair))]
        + [pl.BlockSpec((1, 3, LANES), lambda pair: (pair, 0, 0))]
        + [whole(table.shape) for table in tables],
        out_specs=[slot_single] * slots
        + [
            single,
            pl.BlockSpec((1, 8, rows), lambda pair: (pair, 0, 0)),
            trio,
        ],
        out_shape=[jax.ShapeDtypeStruct((slot_rows, pairs * LANES), low)] * slots
        + [
            jax.ShapeDtypeStruct((rows, pairs * LANES), full),
            jax.ShapeDtypeStruct((pairs, 8, rows), full),
            jax.ShapeDtypeStruct((rows, width), low),
        ],
        scratch_shapes=[pltpu.VMEM((rows, 2 * LANES), low)],
        compiler_params=pltpu.CompilerParams(vmem_limit_bytes=52 * 2**20),
        cost_estimate=pl.CostEstimate(flops=0, bytes_accessed=0, transcendentals=0),
        name="attend",
    )(order, *normed, weight, bias, *tables)
    return (results[:slots], *results[slots:])


def attend_back(order, rotated, grads, fine, totals, tables, ctx_count, tp_count):
    slots = len(grads)
    rows, width = rotated.shape
    slot_rows = rows // slots
    pairs = width // (3 * LANES)
    trio = pl.BlockSpec((rows, 3 * LANES), lambda pair: (0, pair))
    single = pl.BlockSpec((rows, LANES), lambda pair: (0, pair))
    slot_trio = pl.BlockSpec((slot_rows, 3 * LANES), lambda pair: (0, pair))
    slot_single = pl.BlockSpec((slot_rows, LANES), lambda pair: (0, pair))
    results = pl.pallas_call(
        functools.partial(attend_back_kernel, ctx_count, tp_count, slots),
        grid=(pairs,),
        in_specs=[pl.BlockSpec(memory_space=pltpu.SMEM), trio]
        + [slot_single] * slots
        + [single, pl.BlockSpec((1, 8, rows), lambda pair: (pair, 0, 0))]
        + [whole(table.shape) for table in tables],
        out_specs=[slot_trio] * slots + [pl.BlockSpec((1, 8, LANES), lambda pair: (pair, 0, 0))],
        out_shape=[jax.ShapeDtypeStruct((slot_rows, width), low)] * slots
        + [jax.ShapeDtypeStruct((pairs, 8, LANES), full)],
        scratch_shapes=[
            pltpu.VMEM((2, rows, 2 * LANES), low),
            pltpu.VMEM((rows, 2 * LANES), low),
            pltpu.VMEM((2, LANES, rows), low),
            pltpu.VMEM((2, rows, LANES), low),
            pltpu.VMEM((8, rows), full),
            pltpu.VMEM((LANES, rows), full),
            pltpu.VMEM((rows, LANES), full),
            pltpu.VMEM((rows, LANES), full),
            pltpu.VMEM((rows, LANES), full),
        ],
        compiler_params=pltpu.CompilerParams(vmem_limit_bytes=52 * 2**20),
        cost_estimate=pl.CostEstimate(flops=0, bytes_accessed=0, transcendentals=0),
        name="attend_back",
    )(order, rotated, *grads, fine, totals, *tables)
    return (results[:slots], results[slots])


def cut_kernel(ctx_count, with_heads, ctx_ref, *refs):
    gate_up_ref, down_ref, sent_ref = refs[-3:]
    units = down_ref.shape[1] // ctx_count
    for kind in range(3):
        weight = down_ref[...] if kind == 2 else gate_up_ref[kind]
        turned = jnp.transpose(weight.astype(full)).astype(low)
        for place in range(ctx_count):
            sent_ref[ctx_ref[0] ^ place, kind * units : (kind + 1) * units, :] = turned[
                place * units : (place + 1) * units
            ]
    if not with_heads:
        return
    qkv_ref, out_weight_ref = refs[:2]
    width = out_weight_ref.shape[1] // ctx_count
    for place in range(ctx_count):
        start = 3 * units
        for kinds in (range(3), (None,)):
            for pair in range(width // LANES):
                columns = slice(place * width + pair * LANES, place * width + (pair + 1) * LANES)
                for kind in kinds:
                    tile = (
                        out_weight_ref[:, columns] if kind is None else qkv_ref[kind, :, columns]
                    )
                    sent_ref[ctx_ref[0] ^ place, start : start + LANES, :] = tile
                    start += LANES


def join_kernel(ctx_count, unit_outs, ctx_ref, *refs):
    parts, outs = refs[:ctx_count], refs[ctx_count:]
    for step in range(ctx_count):
        place = pl.ds(pl.multiple_of((ctx_ref[0] ^ step) * LANES, LANES), LANES)
        start = 0
        for out in outs[:unit_outs]:
            out[:, place] = parts[step][start : start + out.shape[0], :]
            start += out.shape[0]
        for out in outs[unit_outs:]:
            for tile in range(out.shape[1] // LANES):
                out[place, tile * LANES : (tile + 1) * LANES] = parts[step][
                    start : start + LANES, :
                ]
                start += LANES


def join_units_kernel(ctx_count, ctx_ref, *refs):
    parts, (gate_up_ref, down_ref, held) = refs[:ctx_count], refs[-3:]
    units = down_ref.shape[2] // ctx_count
    for kind in range(3):
        for step in range(ctx_count):
            rows = pl.ds(pl.multiple_of((ctx_ref[0] ^ step) * units, 16), units)
            held[rows, :] = parts[step][kind * units : (kind + 1) * units, :]
        turned = jnp.transpose(held[...].astype(full))
        if kind == 2:
            down_ref[0] = turned
        else:
            gate_up_ref[0, :, kind, :] = turned


def join_heads_kernel(ctx_count, ctx_ref, *refs):
    parts, (qkv_ref, out_ref) = refs[:ctx_count], refs[-2:]
    width = out_ref.shape[2] // ctx_count
    for step in range(ctx_count):
        place = (ctx_ref[0] ^ step) * width
        start = parts[step].shape[0] - 4 * width
        for kinds in (range(3), (None,)):
            for pair in range(width // LANES):
                columns = pl.ds(pl.multiple_of(place + pair * LANES, LANES), LANES)
                for kind in kinds:
                    tile = jnp.transpose(parts[step][start : start + LANES, :].astype(full))
                    if kind is None:
                        out_ref[0, :, columns] = tile
                    else:
                        qkv_ref[0, kind, :, columns] = tile
                    start += LANES


def weight_grad_kernel(piece_counts, *refs):
    count = sum(piece_counts)
    lefts, rights, (out_ref, turned_ref) = refs[:count], refs[count : 2 * count], refs[2 * count :]
    rows = lefts[0].shape[0]

    @pl.when(pl.program_id(0) == 0)
    def turn():
        start = first = 0
        for pieces in piece_counts:
            width = lefts[first].shape[1]
            for piece in range(pieces):
                turned = jnp.transpose(lefts[first + piece][...].astype(full)).astype(low)
                turned_ref[start : start + width, piece * rows : (piece + 1) * rows] = turned
            first += pieces
            start += width

    start = first = 0
    for pieces in piece_counts:
        width = lefts[first].shape[1]
        total = None
        for piece in range(pieces):
            product = dot_nn(
                turned_ref[start : start + width, piece * rows : (piece + 1) * rows],
                rights[first + piece][...],
            )
            total = product if total is None else total + product
        out_ref[start : start + width, :] = total.astype(low)
        first += pieces
        start += width


def weight_grads(groups, columns_all=None, start=0, earlier=None):
    lefts = [left for group_lefts, unused in groups for left in group_lefts]
    rights = [right for unused, group_rights in groups for right in group_rights]
    columns = sum(group_lefts[0].shape[1] for group_lefts, unused in groups)
    rows, features = rights[0].shape
    pieces = [len(group_lefts) for group_lefts, unused in groups]
    block = 512
    kept = [] if earlier is None else [earlier]

    def kernel(*refs):
        weight_grad_kernel(pieces, *refs[: 2 * sum(pieces)], *refs[-2:])

    return pl.pallas_call(
        kernel,
        grid=(features // block,),
        in_specs=[pl.BlockSpec(left.shape, lambda i: (0, 0)) for left in lefts]
        + [pl.BlockSpec((rows, block), lambda i: (0, i)) for right in rights]
        + [pl.BlockSpec(memory_space=pl.ANY)] * len(kept),
        out_specs=pl.BlockSpec((columns, block), lambda i: (start // columns, i)),
        out_shape=jax.ShapeDtypeStruct((columns_all or columns, features), low),
        input_output_aliases={2 * sum(pieces): 0} if kept else {},
        scratch_shapes=[pltpu.VMEM((columns, max(pieces) * rows), low)],
        compiler_params=pltpu.CompilerParams(vmem_limit_bytes=56 * 2**20),
        cost_estimate=pl.CostEstimate(
            flops=2 * columns * features * max(pieces) * rows,
            bytes_accessed=columns * features * 4,
            transcendentals=0,
        ),
        name="weight_grads",
    )(*lefts, *rights, *kept)


def start_copies(pairs, sems):
    copies = [
        pltpu.make_async_copy(source, target, sems.at[i])
        for i, (source, target) in enumerate(pairs)
    ]
    for copy in copies:
        copy.start()
    return copies


def weight_pairs(weights_hbm, held_refs):
    units = held_refs[0].shape[0]
    return [
        (weights_hbm.at[i * units : (i + 1) * units, :], held) for i, held in enumerate(held_refs)
    ]


def units_kernel(
    mine_in,
    other_in,
    weights_hbm,
    mine_out,
    other_out,
    mine_gate,
    other_gate,
    mine_up,
    other_up,
    mine_units,
    other_units,
    rows_in,
    gate_w,
    up_w,
    down_w,
    sems,
):
    rows = other_out.shape[0]
    copies = start_copies(
        [(other_in, rows_in.at[:rows, :]), (mine_in, rows_in.at[rows:, :])]
        + weight_pairs(weights_hbm, (gate_w, up_w, down_w)),
        sems,
    )
    copies[0].wait()
    copies[1].wait()
    copies[2].wait()
    gate = dot_nt(rows_in[...], gate_w[...])
    other_gate[...] = gate[:rows]
    mine_gate[...] = gate[rows:]
    copies[3].wait()
    up = dot_nt(rows_in[...], up_w[...])
    other_up[...] = up[:rows]
    mine_up[...] = up[rows:]
    units = (gate / (1.0 + jnp.exp(-gate)) * up).astype(low)
    other_units[...] = units[:rows]
    mine_units[...] = units[rows:]
    copies[4].wait()
    out = dot_nn(units, down_w[...])
    other_out[...] = out[:rows].astype(low)
    mine_out[...] = out[rows:]


def last_units_kernel(
    mine_in,
    other_in,
    mine_grad,
    other_grad,
    weights_hbm,
    mine_out,
    other_out,
    mine_gate,
    other_gate,
    mine_up,
    other_up,
    mine_units,
    other_units,
    rows_in,
    gate_w,
    up_w,
    down_w,
    grad_in,
    sems,
):
    rows = other_out.shape[0]
    copies = start_copies(
        [(other_in, rows_in.at[:rows, :]), (mine_in, rows_in.at[rows:, :])]
        + weight_pairs(weights_hbm, (gate_w, up_w, down_w))
        + [(other_grad, grad_in.at[:rows, :]), (mine_grad, grad_in.at[rows:, :])],
        sems,
    )
    copies[0].wait()
    copies[1].wait()
    copies[2].wait()
    gate = dot_nt(rows_in[...], gate_w[...])
    sigmoid = 1.0 / (1.0 + jnp.exp(-gate))
    copies[3].wait()
    up = dot_nt(rows_in[...], up_w[...])
    copies[4].wait()
    copies[5].wait()
    copies[6].wait()
    grad = dot_nt(grad_in[...], down_w[...])
    silu = gate * sigmoid
    units = (silu * up).astype(low)
    grad_up = (grad * silu).astype(low)
    grad_gate = (grad * up * (sigmoid * (1.0 + gate * (1.0 - sigmoid)))).astype(low)
    other_units[...] = units[:rows]
    mine_units[...] = units[rows:]
    other_up[...] = grad_up[:rows]
    mine_up[...] = grad_up[rows:]
    other_gate[...] = grad_gate[:rows]
    mine_gate[...] = grad_gate[rows:]
    out = dot_nn(grad_gate, gate_w[...]) + dot_nn(grad_up, up_w[...])
    other_out[...] = out[:rows].astype(low)
    mine_out[...] = out[rows:]


def units_call(kernel, pieces, weights):
    rows, features = pieces[0].shape
    units = weights.shape[0] // 3
    inside = pl.BlockSpec(memory_space=pltpu.VMEM)
    outside = pl.BlockSpec(memory_space=pl.ANY)
    kept = full if len(pieces) == 2 else low
    out_shape = (
        [jax.ShapeDtypeStruct((rows, features), kind) for kind in (full, low)]
        + [jax.ShapeDtypeStruct((rows, units), kept)] * 4
        + [jax.ShapeDtypeStruct((rows, units), low)] * 2
    )
    held = pltpu.VMEM((2 * rows, features), low)
    done = pl.pallas_call(
        kernel,
        in_specs=[outside] * (len(pieces) + 1),
        out_specs=[inside] * len(out_shape),
        out_shape=out_shape,
        scratch_shapes=[held]
        + [pltpu.VMEM((units, features), low)] * 3
        + [held] * (len(pieces) // 2 - 1)
        + [pltpu.SemaphoreType.DMA((3 + len(pieces),))],
        compiler_params=pltpu.CompilerParams(vmem_limit_bytes=52 * 2**20),
        cost_estimate=pl.CostEstimate(flops=0, bytes_accessed=0, transcendentals=0),
        name="units",
    )(*pieces, weights)
    return (done[:2], done[2:4], done[4:6], done[6:8])


def local_kernel(kernel, ctx, arrays, out_shape):
    inside = pl.BlockSpec(memory_space=pltpu.VMEM)
    return pl.pallas_call(
        kernel,
        in_specs=[pl.BlockSpec(memory_space=pltpu.SMEM)] + [inside] * len(arrays),
        out_specs=jax.tree.map(lambda unused: inside, out_shape),
        out_shape=out_shape,
        compiler_params=pltpu.CompilerParams(vmem_limit_bytes=40 * 2**20),
        cost_estimate=pl.CostEstimate(flops=0, bytes_accessed=0, transcendentals=0),
    )(ctx.reshape(1).astype(jnp.int32), *arrays)


def stacked_kernel(kernel, ctx, arrays, layer, layer_total, shapes, earlier, scratch=()):
    inside = pl.BlockSpec(memory_space=pltpu.VMEM)
    earlier = [] if earlier is None else list(earlier)
    return pl.pallas_call(
        kernel,
        grid=(1,),
        in_specs=[pl.BlockSpec(memory_space=pltpu.SMEM)]
        + [inside] * len(arrays)
        + [pl.BlockSpec(memory_space=pl.ANY)] * len(earlier),
        out_specs=[
            pl.BlockSpec((1,) + shape, lambda i, rank=len(shape): (layer,) + (0,) * rank)
            for shape in shapes
        ],
        out_shape=[jax.ShapeDtypeStruct((layer_total,) + shape, full) for shape in shapes],
        input_output_aliases={1 + len(arrays) + i: i for i in range(len(earlier))},
        scratch_shapes=list(scratch),
        compiler_params=pltpu.CompilerParams(vmem_limit_bytes=40 * 2**20),
        cost_estimate=pl.CostEstimate(flops=0, bytes_accessed=0, transcendentals=0),
    )(ctx.reshape(1).astype(jnp.int32), *arrays, *earlier)


def tied(first, second):
    return lax.optimization_barrier((first, second))


class Group:
    def __init__(self, width, hidden_width, depth, rows):
        self.ctx_count = lax.axis_size("ctx")
        self.tp_count = lax.axis_size("tp")
        self.shard_count = lax.axis_size("shard")
        self.ctx = lax.axis_index("ctx")
        self.tp = lax.axis_index("tp")
        self.paired = (
            self.ctx_count == 4
            and self.shard_count in (2, 4)
            and self.tp_count == 2
            and width % LANES == 0
            and hidden_width % 16 == 0
            and depth == LANES
            and rows % 32 == 0
        )

    def order(self):
        places = jnp.arange(self.ctx_count * self.tp_count, dtype=jnp.int32)
        if not self.paired:
            return places
        away = (places // self.tp_count) ^ self.ctx
        return away * self.tp_count + ((places % self.tp_count) ^ self.tp)

    def across(self, value, step):
        return lax.ppermute(value, "ctx", [(i, i ^ step) for i in range(self.ctx_count)])

    def swap(self, value):
        return lax.ppermute(value, "tp", [(0, 1), (1, 0)])

    def send_rows(self, own):
        if not self.paired:
            return [lax.all_gather(own, ("ctx", "tp"), axis=0, tiled=True)]
        return [own, self.across(own, 1), self.across(own, 2)]

    def receive_rows(self, arrived, work):
        if not self.paired:
            return [work((arrived[0],), 0)[0]]
        own, first, second = arrived
        half = own.shape[0] // 2
        far_top = self.across(first[:half], 2)
        far_end = self.across(second[half:], 1)
        results = []
        behind = None
        for step in range(4):
            here = (own, first, second, None)[step]
            if step == 3:
                here = jnp.concatenate([far_top, far_end], axis=0)
            if behind is not None:
                here = tied(here, behind)[0]
            done, behind = work((here, self.swap(here)), step)
            results.append(done)
        return results

    def receive_pieces(self, arrived):
        slots = self.receive_rows(arrived, lambda pieces, slot: (pieces, None))
        return [piece for pieces in slots for piece in pieces]

    def gather_direct(self, own):
        if not self.paired:
            return self.send_rows(own)
        slots = [self.across(own, step) if step else own for step in range(4)]
        return [piece for here in slots for piece in (here, self.swap(here))]

    def chip_sums(self, pieces):
        if not self.paired:
            return pieces
        return [
            mine + self.swap(other.astype(low)).astype(full)
            for mine, other in zip(pieces[::2], pieces[1::2])
        ]

    def reduce_rows(self, sums, first_fill=None, second_fill=None):
        if not self.paired:
            return lax.psum_scatter(
                sums[0].astype(low), ("ctx", "tp"), scatter_dimension=0, tiled=True
            ).astype(full)
        own, first, second, far = sums
        half = own.shape[0] // 2
        far = far.astype(low)
        early = [
            self.across(far[:half], 1),
            self.across(far[half:], 2),
            self.across(first[:half].astype(low), 1),
            self.across(second[half:].astype(low), 2),
        ]
        if first_fill is not None:
            early, first_fill = tied(early, first_fill)
        far_top, far_end, first_top, second_end = [part.astype(full) for part in early]
        late = [(second[:half] + far_top).astype(low), (first[half:] + far_end).astype(low)]
        if second_fill is not None:
            late, first_fill = tied(late, first_fill)
        late = [self.across(late[0], 2), self.across(late[1], 1)]
        if second_fill is not None:
            fill = second_fill(first_fill)
            late, fill = tied(late, fill)
        second_top, first_end = [part.astype(full) for part in late]
        result = own + jnp.concatenate([first_top + second_top, first_end + second_end], axis=0)
        return result if second_fill is None else (result, fill)

    def send_sums(self, sums):
        if not self.paired:
            return sums
        return [sums[0]] + [self.across(sums[step].astype(low), step) for step in range(1, 4)]

    def add_sums(self, arrived):
        if not self.paired:
            return self.reduce_rows(arrived)
        return sum([part.astype(full) for part in arrived[1:]], arrived[0])

    def both_halves(self, value):
        if not self.paired:
            return lax.all_gather(value, "tp", axis=0, tiled=True)
        other = self.swap(value)
        return jnp.where(
            self.tp == 0,
            jnp.concatenate([value, other], axis=0),
            jnp.concatenate([other, value], axis=0),
        )

    def exchange(self, value, axis, count):
        parts = [value] + [
            lax.ppermute(value, axis, [(i, i ^ step) for i in range(count)])
            for step in range(1, count)
        ]
        while len(parts) > 1:
            parts = [left + right for left, right in zip(parts[::2], parts[1::2])]
        return parts[0]

    def total(self, norms, biases):
        if not self.paired:
            return (lax.psum(norms, ("shard", "ctx", "tp")), lax.psum(biases, ("shard", "ctx")))
        flat = self.exchange(norms.reshape(-1, LANES), "tp", self.tp_count)
        count = flat.shape[0]
        flat = jnp.concatenate([flat, biases.reshape(-1, LANES)], axis=0)
        flat = self.exchange(flat, "ctx", self.ctx_count)
        flat = self.exchange(flat, "shard", self.shard_count)
        return (flat[:count].reshape(norms.shape), flat[count:].reshape(biases.shape))


    def send_heads(self, qkv, out):
        size = out.shape[1] // self.ctx_count
        parts = []
        for step in range(self.ctx_count):
            start = (self.ctx ^ step) * size
            piece = jnp.concatenate(
                [
                    pair_columns(lax.dynamic_slice_in_dim(qkv, start, size, 2)),
                    lax.dynamic_slice_in_dim(out, start, size, 1),
                ],
                axis=1,
            )
            piece = jnp.moveaxis(piece.reshape(LANES, -1, LANES), 1, 0).reshape(-1, LANES)
            parts.append(self.across(piece, step) if step else piece)
        return parts

    def cut_layer(self, heads, gate_up, down):
        arrays = [jnp.moveaxis(gate_up, 1, 0), down]
        rows = 3 * down.shape[1] // self.ctx_count
        if heads is not None:
            qkv, out = heads
            arrays = [jnp.moveaxis(qkv, 1, 0), out] + arrays
            rows += 4 * out.shape[1] // self.ctx_count
        return local_kernel(
            functools.partial(cut_kernel, self.ctx_count, heads is not None),
            self.ctx,
            arrays,
            jax.ShapeDtypeStruct((self.ctx_count, rows, LANES), low),
        )

    def send_cut(self, cut):
        return [self.across(cut[k], k) if k else cut[k] for k in range(self.ctx_count)]

    def join_parts(self, parts, units, columns):
        features = LANES * self.ctx_count
        return local_kernel(
            functools.partial(join_kernel, self.ctx_count, len(units)),
            self.ctx,
            parts,
            [jax.ShapeDtypeStruct((size, features), low) for size in units]
            + [jax.ShapeDtypeStruct((features, size), low) for size in columns],
        )

    def split_send(self, value):
        if not self.paired:
            return [value]
        parts = []
        for step in range(self.ctx_count):
            piece = lax.dynamic_slice_in_dim(value, (self.ctx ^ step) * LANES, LANES, 1)
            parts.append(self.across(piece, step) if step else piece)
        return parts

    def join_units(self, parts, tp_units, layer, layer_total, earlier):
        units = tp_units // self.ctx_count
        if not self.paired:
            gate_up = parts[0][: 2 * units].reshape(2, units, -1)
            gate_up = self.spread(gate_up, 2, 1)
            down = self.spread(parts[0][2 * units : 3 * units], 1, 0)
            values = (jnp.transpose(gate_up, (2, 0, 1)), jnp.transpose(down))
            return self.stack_layer(values, layer, layer_total, earlier)
        return stacked_kernel(
            functools.partial(join_units_kernel, self.ctx_count),
            self.ctx,
            parts,
            layer,
            layer_total,
            [(LANES, 2, tp_units), (LANES, tp_units)],
            earlier,
            [pltpu.VMEM((tp_units, LANES), low)],
        )

    def join_heads(self, parts, width, layer, layer_total, earlier):
        if not self.paired:
            columns = 4 * (-(-width // LANES) * LANES)
            qkv = unpair_columns(parts[0][-columns : -columns // 4].T, width)
            out = parts[0][-columns // 4 :].T[:, :width]
            values = (jnp.swapaxes(self.spread(qkv, 0, 2), 0, 1), self.spread(out, 0, 1))
            return self.stack_layer(values, layer, layer_total, earlier)
        tp_width = width * self.ctx_count
        return stacked_kernel(
            functools.partial(join_heads_kernel, self.ctx_count),
            self.ctx,
            parts,
            layer,
            layer_total,
            [(3, LANES, tp_width), (LANES, tp_width)],
            earlier,
        )


    def stack_layer(self, values, layer, layer_total, earlier):
        if earlier is None:
            earlier = [jnp.zeros((layer_total,) + value.shape, full) for value in values]
        return [stack.at[layer].set(value.astype(full)) for stack, value in zip(earlier, values)]

    def spread(self, value, split_axis, join_axis):
        return lax.all_to_all(value, "ctx", split_axis, join_axis, tiled=True)

    def spread_layer(self, qkv, out, gate_up, down):
        gate_up = self.spread(jnp.transpose(gate_up, (1, 2, 0)), 1, 2)
        return (
            over_shard(pair_columns(self.spread(qkv, 2, 0)), 0),
            over_shard(pad_columns(self.spread(out, 1, 0)), 0),
            over_shard(gate_up.reshape(-1, gate_up.shape[2]), 1),
            over_shard(self.spread(jnp.transpose(down), 0, 1), 1),
        )


def pair_columns(weight):
    width = weight.shape[-1]
    pairs = -(-width // LANES)
    if pairs * LANES != width:
        weight = jnp.pad(weight, [(0, 0)] * (weight.ndim - 1) + [(0, pairs * LANES - width)])
    lead = weight.shape[:-2]
    weight = weight.reshape(lead + (3, pairs, LANES))
    return jnp.moveaxis(weight, -2, -3).reshape(lead + (pairs * 3 * LANES,))


def unpair_columns(value, width):
    lead = value.shape[:-1]
    pairs = value.shape[-1] // (3 * LANES)
    value = jnp.moveaxis(value.reshape(lead + (pairs, 3, LANES)), -3, -2)
    return value.reshape(lead + (3, pairs * LANES))[..., :width]


def pad_columns(weight):
    width = weight.shape[-1]
    filled = -(-width // LANES) * LANES
    return weight if filled == width else jnp.pad(weight, [(0, 0), (0, filled - width)])


def sum_dots(groups):
    return jnp.concatenate([dot_tn(lefts[0], rights[0]) for lefts, rights in groups]).astype(low)


def flat_pieces(slots_done):
    return [[piece for pieces in kind for piece in pieces] for kind in zip(*slots_done)]


def unit_grads(rows_in, gate, up, weights):
    gate_weight, up_weight, down = weights
    grad_hidden = dot_nt(rows_in, down)
    sigmoid = jax.nn.sigmoid(gate)
    grad_gate = (grad_hidden * up * (sigmoid * (1.0 + gate * (1.0 - sigmoid)))).astype(low)
    grad_up = (grad_hidden * (gate * sigmoid)).astype(low)
    return (grad_gate, grad_up, dot_nn(grad_gate, gate_weight) + dot_nn(grad_up, up_weight))


def over_shard(value, axis):
    return lax.all_gather(value, "shard", axis=axis, tiled=True)


def sum_shard(value, axis):
    return lax.psum_scatter(value, "shard", scatter_dimension=axis, tiled=True)


def body(
    tokens,
    cotangent,
    lengths,
    norm_gain,
    norm_bias,
    input_bias,
    input_projection,
    output_projection,
    gate_up_weight,
    down_weight,
):
    held_rows = tokens.shape[0]
    layer_total = input_projection.shape[0]
    tp_width = input_bias.shape[2]
    ctx_count, tp_count = lax.axis_size("ctx"), lax.axis_size("tp")
    width = tp_width // ctx_count
    hidden_width = down_weight.shape[2] // ctx_count
    rows = held_rows // tp_count
    group = Group(width, hidden_width, input_projection.shape[1], rows)
    seq_ids, length, offset = row_meta(lengths[0], held_rows)
    positions = (
        jnp.arange(ctx_count, dtype=jnp.int32)[:, None] * length[None, :] + offset[None, :]
    ).reshape(-1)
    lane = jnp.arange(LANES, dtype=jnp.int32)[None, :]
    same = lane == seq_ids[:, None]
    named = lane < lengths.shape[1]
    query_mark = jnp.where(named & ~same, blocked, 0.0).astype(low)
    key_mark = jnp.where(same, 1.0, 0.0).astype(low)
    tables = wide_rotary_tables(positions) + (query_mark, key_mark)
    order = group.order()
    bias_own = lax.dynamic_slice_in_dim(input_bias, group.ctx * width, width, 2)
    bias_pairs = pair_columns(bias_own).reshape(layer_total, -1, 3, LANES)

    def own_rows(value):
        return lax.dynamic_slice_in_dim(value, group.tp * rows, rows, 0)

    def sources(index):
        return (
            input_projection[index],
            output_projection[index],
            gate_up_weight[index],
            down_weight[index],
        )

    def norm_one(index, stream):
        scaled, inverse, normed = norm_parts(stream, norm_gain[index, 0], norm_bias[index, 0])
        return (scaled, inverse, group.send_rows(normed.astype(low)))

    stream = own_rows(tokens).astype(full)
    qkv_columns = 3 * width

    def split_heads(heads_full):
        return (heads_full, heads_full[:, qkv_columns:])

    def split_units(units_full):
        return (
            units_full[:hidden_width],
            units_full[hidden_width : 2 * hidden_width],
            units_full[2 * hidden_width :],
        )

    if group.paired:
        (heads_part,) = group.join_parts(
            group.send_heads(*sources(0)[:2]), [], [qkv_columns + width]
        )
        heads_full = over_shard(heads_part, 0)
        first_norm = norm_one(0, stream)
        cut = tied(group.cut_layer(None, *sources(0)[2:]), first_norm[2])[0]
        (units_part,) = group.join_parts(group.send_cut(cut), [3 * hidden_width], [])
        weights = [split_heads(heads_full) + (over_shard(units_part, 1),)]
    else:
        first_norm = norm_one(0, stream)
        weights = []
        for index in range(layer_total):
            qkv_full, out_full, gate_up_full, down_full = group.spread_layer(*sources(index))
            weights.append(
                (qkv_full, out_full)
                + (jnp.concatenate([gate_up_full, down_full], axis=0),)
            )

    saved = []
    last_branch = None
    for index in range(layer_total):
        last = index + 1 == layer_total
        qkv_weight, out_weight, units_full = weights[index]
        gate_weight, up_weight, down = split_units(units_full)
        scaled_one, inverse_one, arrived = norm_one(index, stream) if index else first_norm
        normed_one = group.receive_pieces(arrived)
        travel = None
        if group.paired and not last:
            travel = group.send_cut(
                tied(
                    group.cut_layer(sources(index + 1)[:2], *sources(index + 1)[2:]), normed_one
                )[0]
            )
        heads, fine, totals, rotated = attend(
            order, normed_one, qkv_weight, bias_pairs[index], tables, ctx_count, tp_count
        )
        if travel is not None:
            heads, travel = tied(heads, travel)
        if group.paired and not last:
            units_part, heads_part = group.join_parts(
                travel, [3 * hidden_width], [qkv_columns + width]
            )
            heads = tied(heads, (units_part, heads_part))[0]
            weights.append(
                split_heads(over_shard(heads_part, 0)) + (over_shard(units_part, 1),)
            )
        attention = group.reduce_rows(
            group.chip_sums([dot_nt(rows_in, out_weight) for rows_in in heads])
        )
        middle = stream + attention
        scaled_two, inverse_two, normed_two = norm_parts(
            middle, norm_gain[index, 1], norm_bias[index, 1]
        )

        def forward_units(pieces, slot):
            if group.paired:
                feeds, gates, ups, hidden = units_call(units_kernel, pieces, units_full)
                return ((pieces, gates, ups, hidden, feeds), feeds)
            gates = [dot_nt(rows_in, gate_weight) for rows_in in pieces]
            ups = [dot_nt(rows_in, up_weight) for rows_in in pieces]
            hidden = [(jax.nn.silu(gate) * up).astype(low) for gate, up in zip(gates, ups)]
            feeds = [dot_nn(units, down) for units in hidden]
            return ((pieces, gates, ups, hidden, feeds), hidden)

        def last_units(pieces, slot):
            size = len(pieces)
            grads = last_branch[slot * size : (slot + 1) * size]
            if group.paired:
                partials, grad_gates, grad_ups, hidden = units_call(
                    last_units_kernel, (*pieces, *grads), units_full
                )
                return ((pieces, grad_gates, grad_ups, hidden, partials), partials)
            gate, up = dot_nt(pieces[0], gate_weight), dot_nt(pieces[0], up_weight)
            hidden = (jax.nn.silu(gate) * up).astype(low)
            grad_gate, grad_up, partial = unit_grads(
                grads[0], gate, up, (gate_weight, up_weight, down)
            )
            return ((pieces, [grad_gate], [grad_up], [hidden], [partial]), None)

        arrived = group.send_rows(normed_two.astype(low))
        if last:
            if last_branch is None:
                last_branch = group.receive_pieces(group.send_rows(own_rows(cotangent)))
            slots_done = group.receive_rows(arrived, last_units)
            normed_two, gates, ups, hidden, last_partials = flat_pieces(slots_done)
        else:
            pieces = lax.optimization_barrier(group.receive_pieces(arrived))
            if index + 2 == layer_total:
                last_branch = group.gather_direct(tied(own_rows(cotangent), pieces)[0])
            size = len(pieces) // (4 if group.paired else 1)
            slots_done = [
                forward_units(pieces[i : i + size], i // size)[0]
                for i in range(0, len(pieces), size)
            ]
            normed_two, gates, ups, hidden, feeds = flat_pieces(slots_done)
            feeds = group.chip_sums(feeds)
            if index + 2 == layer_total:
                feeds, last_branch = tied(feeds, last_branch)
            if group.paired:
                feeds = tied(feeds, weights[index + 1][0])[0]
            stream = middle + group.reduce_rows(feeds)
        saved.append(
            (
                scaled_one,
                inverse_one,
                normed_one,
                heads,
                fine,
                totals,
                rotated,
                scaled_two,
                inverse_two,
                normed_two,
                gates,
                ups,
                hidden,
            )
        )

    grad_stream = own_rows(cotangent).astype(full)
    norm_list = [None] * layer_total
    input_bias_list = [None] * layer_total
    head_stacks = None
    unit_stacks = None
    waiting = None
    for index in reversed(range(layer_total)):
        last = index + 1 == layer_total
        (
            scaled_one,
            inverse_one,
            normed_one,
            heads,
            fine,
            totals,
            rotated,
            scaled_two,
            inverse_two,
            normed_two,
            gates,
            ups,
            hidden,
        ) = saved[index]
        qkv_weight, out_weight, units_full = weights[index]
        gate_weight, up_weight, down = split_units(units_full)


        def backward_units(pieces, slot):
            grad_gates, grad_ups, partials = [], [], []
            for place, rows_in in enumerate(pieces, slot * len(pieces)):
                grad_gate, grad_up, partial = unit_grads(
                    rows_in, gates[place], ups[place], (gate_weight, up_weight, down)
                )
                grad_gates.append(grad_gate)
                grad_ups.append(grad_up)
                partials.append(partial)
            return ((pieces, grad_gates, grad_ups, partials), (grad_gates, grad_ups))

        if last:
            branch, grad_gates, grad_ups, partials = last_branch, gates, ups, last_partials
        else:
            slots_done = group.receive_rows(
                group.send_rows(grad_stream.astype(low)), backward_units
            )
            branch, grad_gates, grad_ups, partials = flat_pieces(slots_done)
        sums = group.chip_sums(partials)
        (branch, grad_gates, grad_ups, hidden), unused = tied(
            (branch, grad_gates, grad_ups, hidden), sums
        )
        if group.paired:
            down_grad = weight_grads([(hidden, branch)], 3 * hidden_width, 2 * hidden_width)
            grad_normed_two, units_grad = group.reduce_rows(
                sums,
                down_grad,
                lambda earlier: weight_grads(
                    [(grad_gates, normed_two), (grad_ups, normed_two)],
                    3 * hidden_width,
                    0,
                    earlier,
                ),
            )
        else:
            units_grad = sum_dots(
                [(grad_gates, normed_two), (grad_ups, normed_two), (hidden, branch)]
            )
            grad_normed_two = group.reduce_rows(sums)
        units_part = sum_shard(units_grad, 1)
        if last:
            feeds = group.chip_sums([dot_nn(units, down) for units in hidden])
        grad_input_two, gain_two, bias_two = norm_back(
            grad_normed_two, scaled_two, inverse_two, norm_gain[index, 1]
        )
        grad_middle = grad_stream + grad_input_two
        branch = group.receive_pieces(group.send_rows(grad_middle.astype(low)))
        grad_heads = [dot_nn(rows_in, out_weight).astype(low) for rows_in in branch]
        if last:
            travel = group.send_sums(tied(feeds, grad_heads)[0])
        else:
            travel = group.split_send(tied(waiting, grad_heads)[0])
        grad_qkv, bias_sums = attend_back(
            order, rotated, grad_heads, fine, totals, tables, ctx_count, tp_count
        )
        grad_qkv, travel, branch = lax.optimization_barrier((grad_qkv, travel, branch))
        if last:
            result = (middle + group.add_sums(travel)).astype(low)
        else:
            unit_stacks = group.join_units(
                travel, hidden_width * ctx_count, index + 1, layer_total, unit_stacks
            )
            head_stacks = group.join_heads(travel, width, index + 1, layer_total, head_stacks)
        sums = group.chip_sums(
            [dot_nt(rows_in, qkv_weight[:, : rows_in.shape[1]]) for rows_in in grad_qkv]
        )
        if group.paired:
            grad_normed_one, heads_grad = group.reduce_rows(
                sums,
                (grad_qkv, branch),
                lambda held: weight_grads([(held[0], normed_one), (heads, held[1])]),
            )
        else:
            heads_grad = sum_dots([(grad_qkv, normed_one), (heads, branch)])
            grad_normed_one = group.reduce_rows(sums)
        grad_normed_one = tied(grad_normed_one, units_part)[0]
        heads_part = sum_shard(heads_grad, 1)
        if index:
            waiting = jnp.concatenate([units_part, heads_part], axis=0)
        bias_sums = bias_sums[:, :3, :].transpose(1, 0, 2).reshape(3, -1)[:, :width]
        input_bias_list[index] = lax.dynamic_update_slice_in_dim(
            jnp.zeros((3, tp_width), full), bias_sums, group.ctx * width, 1
        )
        grad_input_one, gain_one, bias_one = norm_back(
            grad_normed_one, scaled_one, inverse_one, norm_gain[index, 0]
        )
        grad_stream = grad_middle + grad_input_one
        norm_list[index] = jnp.stack([gain_one, gain_two, bias_one, bias_two])
    unit_stacks = group.join_units(
        group.split_send(units_part), hidden_width * ctx_count, 0, layer_total, unit_stacks
    )
    norm_total, bias_total = group.total(jnp.stack(norm_list), jnp.stack(input_bias_list))
    result = group.both_halves(result)
    tokens_grad = group.both_halves(grad_stream)
    heads_part = tied(heads_part, (unit_stacks, norm_total, bias_total, result, tokens_grad))[0]
    head_stacks = group.join_heads(
        group.split_send(heads_part), width, 0, layer_total, head_stacks
    )
    return (
        result,
        tokens_grad,
        norm_total[:, :2],
        norm_total[:, 2:],
        bias_total,
        jnp.moveaxis(head_stacks[0], 1, 2),
        head_stacks[1],
        unit_stacks[0],
        unit_stacks[1],
    )


def solution(mesh):
    in_specs = (
        P(("shard", "ctx"), None),
        P(("shard", "ctx"), None),
        P("shard", None),
        P(),
        P(),
        P(None, None, "tp"),
        P(None, ("shard", "ctx"), None, "tp"),
        P(None, ("shard", "ctx"), "tp"),
        P(None, ("shard", "ctx"), None, "tp"),
        P(None, ("shard", "ctx"), "tp"),
    )
    out_specs = (
        P(("shard", "ctx"), None),
        P(("shard", "ctx"), None),
        P(),
        P(),
        P(None, None, "tp"),
        P(None, ("shard", "ctx"), None, "tp"),
        P(None, ("shard", "ctx"), "tp"),
        P(None, ("shard", "ctx"), None, "tp"),
        P(None, ("shard", "ctx"), "tp"),
    )
    return jax.shard_map(body, mesh=mesh, in_specs=in_specs, out_specs=out_specs, check_vma=False)
```

```python
import functools
import math

import jax
import jax.numpy as jnp
from jax import lax
from jax.experimental import pallas as pl
from jax.experimental.pallas import tpu as pltpu
from jax.sharding import PartitionSpec as P

HEAD = 64
ROT = 16
LANES = 128

norm_eps = 1e-05
rotary_base = 10000.0
blocked = -(2.0**100)
low = jnp.bfloat16
full = jnp.float32


def row_meta(seq_lengths, row_count):
    seq_ends = jnp.cumsum(seq_lengths, dtype=jnp.int32)
    row_index = jnp.arange(row_count, dtype=jnp.int32)
    seq_ids = jnp.sum(
        (row_index[:, None] >= seq_ends[None, :]).astype(jnp.int32), axis=1, dtype=jnp.int32
    )
    one_hot = (
        seq_ids[:, None] == jnp.arange(seq_lengths.shape[0], dtype=jnp.int32)[None, :]
    ).astype(jnp.int32)
    seq_start = jnp.sum(one_hot * (seq_ends - seq_lengths)[None, :], axis=1, dtype=jnp.int32)
    length = jnp.sum(one_hot * seq_lengths[None, :], axis=1, dtype=jnp.int32)
    return (seq_ids, length, row_index - seq_start)


def wide_rotary_tables(positions):
    half_rot = ROT // 2
    frequency = rotary_base ** (-(2.0 * jnp.arange(half_rot, dtype=full)) / ROT)
    lane = jnp.arange(LANES, dtype=jnp.int32) % HEAD
    lane_frequency = jnp.where(lane < ROT, jnp.tile(frequency, LANES // half_rot), 0.0)
    sign = jnp.where(lane < half_rot, -1.0, 1.0)
    angles = positions.astype(full)[:, None] * lane_frequency[None, :]
    return (jnp.cos(angles), jnp.sin(angles) * sign[None, :])


def norm_parts(stream, gain_row, bias_row):
    row_mean = jnp.mean(stream, axis=-1, keepdims=True)
    centered = stream - row_mean
    variance = jnp.mean(centered * centered, axis=-1, keepdims=True)
    inverse = lax.rsqrt(variance + norm_eps)
    scaled = centered * inverse
    return (scaled, inverse, scaled * gain_row + bias_row)


def norm_back(grad_normed, scaled, inverse, gain_row):
    grad_scaled = grad_normed * gain_row
    inner = (
        grad_scaled
        - jnp.mean(grad_scaled, axis=-1, keepdims=True)
        - scaled * jnp.mean(grad_scaled * scaled, axis=-1, keepdims=True)
    )
    return (inverse * inner, jnp.sum(grad_normed * scaled, axis=0), jnp.sum(grad_normed, axis=0))


def dot_nn(left, right):
    return lax.dot_general(left, right, (((1,), (0,)), ((), ())), preferred_element_type=full)


def dot_nt(left, right):
    return lax.dot_general(left, right, (((1,), (1,)), ((), ())), preferred_element_type=full)


def dot_tn(left, right):
    return lax.dot_general(left, right, (((0,), (0,)), ((), ())), preferred_element_type=full)


def partner(values, lane):
    near = pltpu.roll(values, LANES - ROT // 2, 1)
    far = pltpu.roll(values, ROT // 2, 1)
    return jnp.where(lane % HEAD < ROT // 2, near, far)


def attend_kernel(ctx_count, tp_count, slots, order_ref, *refs):
    normed_refs = refs[:slots]
    weight_ref, bias_ref, cos_ref, sin_ref, query_mark_ref, key_mark_ref = refs[slots : slots + 6]
    out_refs = refs[slots + 6 : 2 * slots + 6]
    fine_ref, total_ref, rotated_ref, key_wide = refs[2 * slots + 6 :]
    rows_all = rotated_ref.shape[0]
    block = rows_all // ctx_count
    part = block // tp_count
    slot_parts = ctx_count * tp_count // slots
    lane_part = lax.broadcasted_iota(jnp.int32, (part, LANES), 1)
    to_exponent = float(HEAD) ** (-0.5) * math.log2(math.e)

    for place in range(ctx_count * tp_count):
        slot, start = place // slot_parts, place % slot_parts * part
        source = slice(start, start + part)
        target = pl.ds(pl.multiple_of(order_ref[place] * part, part), part)
        mark = pl.ds(pl.multiple_of(lax.rem(order_ref[place], tp_count) * part, part), part)
        cosine = cos_ref[target, :]
        sine = sin_ref[target, :]
        joined = dot_nn(normed_refs[slot][source, :], weight_ref[...])
        for kind in range(3):
            columns = slice(kind * LANES, (kind + 1) * LANES)
            values = joined[:, columns] + bias_ref[0, kind : kind + 1, :]
            if kind < 2:
                values = values * cosine + partner(values, lane_part) * sine
            rotated_ref[target, columns] = values.astype(low)
        key_wide[target, :LANES] = rotated_ref[target, LANES : 2 * LANES]
        key_wide[target, LANES:] = key_mark_ref[mark, :]

    tile = min(256, block)
    lane_tile = lax.broadcasted_iota(jnp.int32, (tile, LANES), 1)
    row_index = lax.broadcasted_iota(jnp.int32, (tile, block), 0)
    column_index = lax.broadcasted_iota(jnp.int32, (tile, block), 1)
    for place in range(ctx_count):
        past = place * block
        for head in range(2):

            def step(sub, unused):
                start = pl.multiple_of(sub * tile, tile)
                rows = pl.ds(pl.multiple_of(past + sub * tile, tile), tile)
                own_lanes = lane_tile // HEAD == head
                query = rotated_ref[rows, :LANES]
                query = jnp.concatenate(
                    [
                        jnp.where(own_lanes, query, jnp.zeros_like(query)),
                        query_mark_ref[pl.ds(start, tile), :],
                    ],
                    axis=1,
                )
                near = dot_nt(query, key_wide[past : past + block, :])
                near = jnp.where(column_index <= row_index + start, near, blocked)
                top = jnp.max(near, axis=1, keepdims=True)
                if past:
                    far = dot_nt(query, key_wide[:past, :])
                    top = jnp.maximum(top, jnp.max(far, axis=1, keepdims=True))
                shift = top * to_exponent
                near = jnp.exp2(near * to_exponent - shift)
                total = jnp.sum(near, axis=1, keepdims=True)
                out = dot_nn(near.astype(low), rotated_ref[past : past + block, 2 * LANES :])
                if past:
                    far = jnp.exp2(far * to_exponent - shift)
                    total = total + jnp.sum(far, axis=1, keepdims=True)
                    out = out + dot_nn(far.astype(low), rotated_ref[:past, 2 * LANES :])
                out = out / total
                fine_ref[rows, :] = jnp.where(own_lanes, out, fine_ref[rows, :])
                log_total = jnp.broadcast_to(shift + jnp.log2(total), (tile, LANES))
                total_ref[0, head : head + 1, rows] = jnp.transpose(log_total)[:1, :]
                return unused

            lax.fori_loop(0, block // tile, step, 0)

    for place in range(ctx_count * tp_count):
        slot, start = place // slot_parts, place % slot_parts * part
        source = pl.ds(pl.multiple_of(order_ref[place] * part, part), part)
        out_refs[slot][start : start + part, :] = fine_ref[source, :].astype(low)


def attend_back_kernel(ctx_count, tp_count, slots, order_ref, rotated_ref, *refs):
    grad_refs = refs[:slots]
    fine_ref, total_ref, cos_ref, sin_ref, query_mark_ref, key_mark_ref = refs[slots : slots + 6]
    out_refs = refs[slots + 6 : 2 * slots + 6]
    (
        sum_ref,
        query_wide,
        key_wide,
        key_turned,
        grad_own,
        row_dots,
        grad_query,
        grad_key,
        grad_value,
        query_rows_grad,
    ) = refs[2 * slots + 6 :]
    rows_all = rotated_ref.shape[0]
    slot_parts = ctx_count * tp_count // slots
    block = rows_all // ctx_count
    part = block // tp_count
    score_scale = float(HEAD) ** (-0.5)
    to_exponent = score_scale * math.log2(math.e)
    lane_block = lax.broadcasted_iota(jnp.int32, (block, LANES), 1)
    lane_part = lax.broadcasted_iota(jnp.int32, (part, LANES), 1)
    head_row = lax.broadcasted_iota(jnp.int32, (LANES, block), 0)

    for place in range(ctx_count * tp_count):
        slot, start = place // slot_parts, place % slot_parts * part
        target = pl.ds(pl.multiple_of(order_ref[place] * part, part), part)
        grad_own[0, target, :] = grad_refs[slot][start : start + part, :]

    def prepare(place, unused):
        rows = pl.ds(pl.multiple_of(place * block, block), block)
        grad = grad_own[0, rows, :]
        product = jnp.transpose(grad.astype(full) * fine_ref[rows, :])
        turned = jnp.transpose(rotated_ref[rows, LANES : 2 * LANES].astype(full))
        query = rotated_ref[rows, :LANES]
        for head in range(2):
            own_lanes = lane_block // HEAD == head
            row_dots[head : head + 1, rows] = jnp.sum(
                product[head * HEAD : (head + 1) * HEAD, :], axis=0, keepdims=True
            )
            key_turned[head, :, rows] = jnp.where(head_row // HEAD == head, turned, 0.0).astype(low)
            query_wide[head, rows, :LANES] = jnp.where(own_lanes, query, jnp.zeros_like(query))
            query_wide[head, rows, LANES:] = query_mark_ref[...]
            grad_own[head, rows, :] = jnp.where(own_lanes, grad, jnp.zeros_like(grad))
        key_wide[rows, :LANES] = rotated_ref[rows, LANES : 2 * LANES]
        key_wide[rows, LANES:] = key_mark_ref[...]
        grad_query[:, rows] = jnp.zeros((LANES, block), full)
        grad_key[rows, :] = jnp.zeros((block, LANES), full)
        grad_value[rows, :] = jnp.zeros((block, LANES), full)
        return unused

    lax.fori_loop(0, ctx_count, prepare, 0)

    small = min(256, block)
    key_index = lax.broadcasted_iota(jnp.int32, (small, small), 0)
    query_index = lax.broadcasted_iota(jnp.int32, (small, small), 1)

    def pair(head, key_rows, query_rows, diagonal):
        query = query_wide[head, query_rows, :]
        scores = dot_nt(key_wide[key_rows, :], query)
        if diagonal:
            scores = jnp.where(key_index <= query_index, scores, blocked)
        probs = jnp.exp2(scores * to_exponent - total_ref[0, head : head + 1, query_rows])
        grad = grad_own[head, query_rows, :]
        grad_probs = dot_nt(rotated_ref[key_rows, 2 * LANES :], grad)
        grad_scores = (probs * (grad_probs - row_dots[head : head + 1, query_rows])).astype(low)
        grad_value[key_rows, :] += dot_nn(probs.astype(low), grad)
        grad_key[key_rows, :] += dot_nn(grad_scores, query[:, :LANES])
        grad_query[:, query_rows] += dot_nn(key_turned[head, :, key_rows], grad_scores)

    for head in range(2):

        def over_keys(key_place, unused, head=head):
            key_rows = pl.ds(pl.multiple_of(key_place * block, block), block)
            for key_part in range(block // small):
                for query_part in range(key_part, block // small):
                    small_rows = [
                        pl.ds(pl.multiple_of(key_place * block + part * small, small), small)
                        for part in (key_part, query_part)
                    ]
                    pair(head, *small_rows, key_part == query_part)

            def over_queries(query_place, inner):
                pair(head, key_rows, pl.ds(pl.multiple_of(query_place * block, block), block), False)
                return inner

            return lax.fori_loop(key_place + 1, ctx_count, over_queries, unused)

        lax.fori_loop(0, ctx_count, over_keys, 0)

    sum_ref[...] = jnp.zeros_like(sum_ref)

    def turn(place, unused):
        rows = pl.ds(pl.multiple_of(place * block, block), block)
        query_rows_grad[rows, :] = jnp.transpose(grad_query[:, rows])
        return unused

    lax.fori_loop(0, ctx_count, turn, 0)

    for place in range(ctx_count * tp_count):
        slot, start = place // slot_parts, place % slot_parts * part
        source = pl.ds(pl.multiple_of(order_ref[place] * part, part), part)
        cosine = cos_ref[source, :]
        sine = sin_ref[source, :]
        values = (
            query_rows_grad[source, :] * score_scale,
            grad_key[source, :] * score_scale,
            grad_value[source, :],
        )
        for kind in range(3):
            value = values[kind]
            if kind < 2:
                value = value * cosine - partner(value, lane_part) * sine
            value = value.astype(low)
            out_refs[slot][start : start + part, kind * LANES : (kind + 1) * LANES] = value
            sum_ref[0, kind : kind + 1, :] += jnp.sum(value.astype(full), axis=0, keepdims=True)


def whole(shape):
    return pl.BlockSpec(shape, lambda pair: (0,) * len(shape))


def attend(order, normed, weight, bias, tables, ctx_count, tp_count):
    slots = len(normed)
    slot_rows, features = normed[0].shape
    rows = slots * slot_rows
    pairs = bias.shape[0]
    width = pairs * 3 * LANES
    trio = pl.BlockSpec((rows, 3 * LANES), lambda pair: (0, pair))
    single = pl.BlockSpec((rows, LANES), lambda pair: (0, pair))
    slot_single = pl.BlockSpec((slot_rows, LANES), lambda pair: (0, pair))
    results = pl.pallas_call(
        functools.partial(attend_kernel, ctx_count, tp_count, slots),
        grid=(pairs,),
        in_specs=[pl.BlockSpec(memory_space=pltpu.SMEM)]
        + [whole((slot_rows, features))] * slots
        + [pl.BlockSpec((features, 3 * LANES), lambda pair: (0, pair))]
        + [pl.BlockSpec((1, 3, LANES), lambda pair: (pair, 0, 0))]
        + [whole(table.shape) for table in tables],
        out_specs=[slot_single] * slots
        + [
            single,
            pl.BlockSpec((1, 8, rows), lambda pair: (pair, 0, 0)),
            trio,
        ],
        out_shape=[jax.ShapeDtypeStruct((slot_rows, pairs * LANES), low)] * slots
        + [
            jax.ShapeDtypeStruct((rows, pairs * LANES), full),
            jax.ShapeDtypeStruct((pairs, 8, rows), full),
            jax.ShapeDtypeStruct((rows, width), low),
        ],
        scratch_shapes=[pltpu.VMEM((rows, 2 * LANES), low)],
        compiler_params=pltpu.CompilerParams(vmem_limit_bytes=52 * 2**20),
        cost_estimate=pl.CostEstimate(
            flops=pairs * rows * rows * LANES * 32, bytes_accessed=0, transcendentals=0
        ),
        name="attend",
    )(order, *normed, weight, bias, *tables)
    return (results[:slots], *results[slots:])


def attend_back(order, rotated, grads, fine, totals, tables, ctx_count, tp_count):
    slots = len(grads)
    rows, width = rotated.shape
    slot_rows = rows // slots
    pairs = width // (3 * LANES)
    trio = pl.BlockSpec((rows, 3 * LANES), lambda pair: (0, pair))
    single = pl.BlockSpec((rows, LANES), lambda pair: (0, pair))
    slot_trio = pl.BlockSpec((slot_rows, 3 * LANES), lambda pair: (0, pair))
    slot_single = pl.BlockSpec((slot_rows, LANES), lambda pair: (0, pair))
    results = pl.pallas_call(
        functools.partial(attend_back_kernel, ctx_count, tp_count, slots),
        grid=(pairs,),
        in_specs=[pl.BlockSpec(memory_space=pltpu.SMEM), trio]
        + [slot_single] * slots
        + [single, pl.BlockSpec((1, 8, rows), lambda pair: (pair, 0, 0))]
        + [whole(table.shape) for table in tables],
        out_specs=[slot_trio] * slots + [pl.BlockSpec((1, 8, LANES), lambda pair: (pair, 0, 0))],
        out_shape=[jax.ShapeDtypeStruct((slot_rows, width), low)] * slots
        + [jax.ShapeDtypeStruct((pairs, 8, LANES), full)],
        scratch_shapes=[
            pltpu.VMEM((2, rows, 2 * LANES), low),
            pltpu.VMEM((rows, 2 * LANES), low),
            pltpu.VMEM((2, LANES, rows), low),
            pltpu.VMEM((2, rows, LANES), low),
            pltpu.VMEM((8, rows), full),
            pltpu.VMEM((LANES, rows), full),
            pltpu.VMEM((rows, LANES), full),
            pltpu.VMEM((rows, LANES), full),
            pltpu.VMEM((rows, LANES), full),
        ],
        compiler_params=pltpu.CompilerParams(vmem_limit_bytes=52 * 2**20),
        cost_estimate=pl.CostEstimate(
            flops=pairs * rows * rows * LANES * 32, bytes_accessed=0, transcendentals=0
        ),
        name="attend_back",
    )(order, rotated, *grads, fine, totals, *tables)
    return (results[:slots], results[slots])


def cut_kernel(ctx_count, with_heads, ctx_ref, *refs):
    gate_up_ref, down_ref, sent_ref = refs[-3:]
    units = down_ref.shape[1] // ctx_count
    for kind in range(3):
        weight = down_ref[...] if kind == 2 else gate_up_ref[kind]
        turned = jnp.transpose(weight.astype(full)).astype(low)
        for place in range(ctx_count):
            sent_ref[ctx_ref[0] ^ place, kind * units : (kind + 1) * units, :] = turned[
                place * units : (place + 1) * units
            ]
    if not with_heads:
        return
    qkv_ref, out_weight_ref = refs[:2]
    width = out_weight_ref.shape[1] // ctx_count
    for place in range(ctx_count):
        start = 3 * units
        for kinds in (range(3), (None,)):
            for pair in range(width // LANES):
                columns = slice(place * width + pair * LANES, place * width + (pair + 1) * LANES)
                for kind in kinds:
                    tile = (
                        out_weight_ref[:, columns] if kind is None else qkv_ref[kind, :, columns]
                    )
                    sent_ref[ctx_ref[0] ^ place, start : start + LANES, :] = tile
                    start += LANES


def join_kernel(ctx_count, unit_outs, ctx_ref, *refs):
    parts, outs = refs[:ctx_count], refs[ctx_count:]
    for step in range(ctx_count):
        place = pl.ds(pl.multiple_of((ctx_ref[0] ^ step) * LANES, LANES), LANES)
        start = 0
        for out in outs[:unit_outs]:
            out[:, place] = parts[step][start : start + out.shape[0], :]
            start += out.shape[0]
        for out in outs[unit_outs:]:
            for tile in range(out.shape[1] // LANES):
                out[place, tile * LANES : (tile + 1) * LANES] = parts[step][
                    start : start + LANES, :
                ]
                start += LANES


def join_units_kernel(ctx_count, ctx_ref, *refs):
    parts, (gate_up_ref, down_ref, held) = refs[:ctx_count], refs[-3:]
    units = down_ref.shape[2] // ctx_count
    for kind in range(3):
        for step in range(ctx_count):
            rows = pl.ds(pl.multiple_of((ctx_ref[0] ^ step) * units, 16), units)
            held[rows, :] = parts[step][kind * units : (kind + 1) * units, :]
        turned = jnp.transpose(held[...].astype(full))
        if kind == 2:
            down_ref[0] = turned
        else:
            gate_up_ref[0, :, kind, :] = turned


def join_heads_kernel(ctx_count, ctx_ref, *refs):
    parts, (qkv_ref, out_ref) = refs[:ctx_count], refs[-2:]
    width = out_ref.shape[2] // ctx_count
    for step in range(ctx_count):
        place = (ctx_ref[0] ^ step) * width
        start = parts[step].shape[0] - 4 * width
        for kinds in (range(3), (None,)):
            for pair in range(width // LANES):
                columns = pl.ds(pl.multiple_of(place + pair * LANES, LANES), LANES)
                for kind in kinds:
                    tile = jnp.transpose(parts[step][start : start + LANES, :].astype(full))
                    if kind is None:
                        out_ref[0, :, columns] = tile
                    else:
                        qkv_ref[0, kind, :, columns] = tile
                    start += LANES


def weight_grad_kernel(piece_counts, *refs):
    count = sum(piece_counts)
    lefts, rights, (out_ref, turned_ref) = refs[:count], refs[count : 2 * count], refs[2 * count :]
    rows = lefts[0].shape[0]

    @pl.when(pl.program_id(0) == 0)
    def turn():
        start = first = 0
        for pieces in piece_counts:
            width = lefts[first].shape[1]
            for piece in range(pieces):
                turned = jnp.transpose(lefts[first + piece][...].astype(full)).astype(low)
                turned_ref[start : start + width, piece * rows : (piece + 1) * rows] = turned
            first += pieces
            start += width

    start = first = 0
    for pieces in piece_counts:
        width = lefts[first].shape[1]
        total = None
        for piece in range(pieces):
            product = dot_nn(
                turned_ref[start : start + width, piece * rows : (piece + 1) * rows],
                rights[first + piece][...],
            )
            total = product if total is None else total + product
        out_ref[start : start + width, :] = total.astype(low)
        first += pieces
        start += width


def weight_grads(groups, columns_all=None, start=0, earlier=None):
    lefts = [left for group_lefts, unused in groups for left in group_lefts]
    rights = [right for unused, group_rights in groups for right in group_rights]
    columns = sum(group_lefts[0].shape[1] for group_lefts, unused in groups)
    rows, features = rights[0].shape
    pieces = [len(group_lefts) for group_lefts, unused in groups]
    block = 512
    kept = [] if earlier is None else [earlier]

    def kernel(*refs):
        weight_grad_kernel(pieces, *refs[: 2 * sum(pieces)], *refs[-2:])

    return pl.pallas_call(
        kernel,
        grid=(features // block,),
        in_specs=[pl.BlockSpec(left.shape, lambda i: (0, 0)) for left in lefts]
        + [pl.BlockSpec((rows, block), lambda i: (0, i)) for right in rights]
        + [pl.BlockSpec(memory_space=pl.ANY)] * len(kept),
        out_specs=pl.BlockSpec((columns, block), lambda i: (start // columns, i)),
        out_shape=jax.ShapeDtypeStruct((columns_all or columns, features), low),
        input_output_aliases={2 * sum(pieces): 0} if kept else {},
        scratch_shapes=[pltpu.VMEM((columns, max(pieces) * rows), low)],
        compiler_params=pltpu.CompilerParams(vmem_limit_bytes=56 * 2**20),
        cost_estimate=pl.CostEstimate(
            flops=2 * columns * features * max(pieces) * rows,
            bytes_accessed=columns * features * 4,
            transcendentals=0,
        ),
        name="weight_grads",
    )(*lefts, *rights, *kept)


def start_weights(weights_hbm, held_refs, sems):
    units = held_refs[0].shape[0]
    copies = [
        pltpu.make_async_copy(weights_hbm.at[i * units : (i + 1) * units, :], held, sems.at[i])
        for i, held in enumerate(held_refs)
    ]
    for copy in copies:
        copy.start()
    return copies


def units_kernel(
    mine_in,
    other_in,
    weights_hbm,
    mine_out,
    other_out,
    mine_gate,
    other_gate,
    mine_up,
    other_up,
    mine_units,
    other_units,
    gate_w,
    up_w,
    down_w,
    sems,
):
    copies = start_weights(weights_hbm, (gate_w, up_w, down_w), sems)
    work = (
        (other_in, other_out, other_gate, other_up, other_units),
        (mine_in, mine_out, mine_gate, mine_up, mine_units),
    )
    for place, (rows_in, out, gate_out, up_out, units_out) in enumerate(work):
        if place == 0:
            copies[0].wait()
        gate = dot_nt(rows_in[...], gate_w[...])
        gate_out[...] = gate
        if place == 0:
            copies[1].wait()
        up = dot_nt(rows_in[...], up_w[...])
        up_out[...] = up
        units = (gate / (1.0 + jnp.exp(-gate)) * up).astype(low)
        units_out[...] = units
        if place == 0:
            copies[2].wait()
        out[...] = dot_nn(units, down_w[...]).astype(out.dtype)


def units_call(pieces, weights):
    rows, features = pieces[0].shape
    units = weights.shape[0] // 3
    inside = pl.BlockSpec(memory_space=pltpu.VMEM)
    out_shape = (
        [jax.ShapeDtypeStruct((rows, features), kind) for kind in (full, low)]
        + [jax.ShapeDtypeStruct((rows, units), full)] * 4
        + [jax.ShapeDtypeStruct((rows, units), low)] * 2
    )
    done = pl.pallas_call(
        units_kernel,
        in_specs=[inside] * 2 + [pl.BlockSpec(memory_space=pl.ANY)],
        out_specs=[inside] * len(out_shape),
        out_shape=out_shape,
        scratch_shapes=[pltpu.VMEM((units, features), low)] * 3 + [pltpu.SemaphoreType.DMA((3,))],
        compiler_params=pltpu.CompilerParams(vmem_limit_bytes=48 * 2**20),
        cost_estimate=pl.CostEstimate(flops=0, bytes_accessed=0, transcendentals=0),
        name="units",
    )(*pieces, weights)
    return (done[:2], done[2:4], done[4:6], done[6:8])


def local_kernel(kernel, ctx, arrays, out_shape):
    inside = pl.BlockSpec(memory_space=pltpu.VMEM)
    return pl.pallas_call(
        kernel,
        in_specs=[pl.BlockSpec(memory_space=pltpu.SMEM)] + [inside] * len(arrays),
        out_specs=jax.tree.map(lambda unused: inside, out_shape),
        out_shape=out_shape,
        compiler_params=pltpu.CompilerParams(vmem_limit_bytes=40 * 2**20),
        cost_estimate=pl.CostEstimate(flops=0, bytes_accessed=0, transcendentals=0),
    )(ctx.reshape(1).astype(jnp.int32), *arrays)


def stacked_kernel(kernel, ctx, arrays, layer, layer_total, shapes, earlier, scratch=()):
    inside = pl.BlockSpec(memory_space=pltpu.VMEM)
    earlier = [] if earlier is None else list(earlier)
    return pl.pallas_call(
        kernel,
        grid=(1,),
        in_specs=[pl.BlockSpec(memory_space=pltpu.SMEM)]
        + [inside] * len(arrays)
        + [pl.BlockSpec(memory_space=pl.ANY)] * len(earlier),
        out_specs=[
            pl.BlockSpec((1,) + shape, lambda i, rank=len(shape): (layer,) + (0,) * rank)
            for shape in shapes
        ],
        out_shape=[jax.ShapeDtypeStruct((layer_total,) + shape, full) for shape in shapes],
        input_output_aliases={1 + len(arrays) + i: i for i in range(len(earlier))},
        scratch_shapes=list(scratch),
        compiler_params=pltpu.CompilerParams(vmem_limit_bytes=40 * 2**20),
        cost_estimate=pl.CostEstimate(flops=0, bytes_accessed=0, transcendentals=0),
    )(ctx.reshape(1).astype(jnp.int32), *arrays, *earlier)


def tied(first, second):
    return lax.optimization_barrier((first, second))


class Group:
    def __init__(self, width, hidden_width, depth, rows):
        self.ctx_count = lax.axis_size("ctx")
        self.tp_count = lax.axis_size("tp")
        self.shard_count = lax.axis_size("shard")
        self.ctx = lax.axis_index("ctx")
        self.tp = lax.axis_index("tp")
        self.paired = (
            self.ctx_count == 4
            and self.shard_count in (2, 4)
            and self.tp_count == 2
            and width % LANES == 0
            and hidden_width % 16 == 0
            and depth == LANES
            and rows % 32 == 0
        )

    def order(self):
        places = jnp.arange(self.ctx_count * self.tp_count, dtype=jnp.int32)
        if not self.paired:
            return places
        away = (places // self.tp_count) ^ self.ctx
        return away * self.tp_count + ((places % self.tp_count) ^ self.tp)

    def across(self, value, step):
        return lax.ppermute(value, "ctx", [(i, i ^ step) for i in range(self.ctx_count)])

    def swap(self, value):
        return lax.ppermute(value, "tp", [(0, 1), (1, 0)])

    def send_rows(self, own):
        if not self.paired:
            return [lax.all_gather(own, ("ctx", "tp"), axis=0, tiled=True)]
        return [own, self.across(own, 1), self.across(own, 2)]

    def receive_rows(self, arrived, work):
        if not self.paired:
            return [work((arrived[0],), 0)[0]]
        own, first, second = arrived
        half = own.shape[0] // 2
        far_top = self.across(first[:half], 2)
        far_end = self.across(second[half:], 1)
        results = []
        behind = None
        for step in range(4):
            here = (own, first, second, None)[step]
            if step == 3:
                here = jnp.concatenate([far_top, far_end], axis=0)
            if behind is not None:
                here = tied(here, behind)[0]
            done, behind = work((here, self.swap(here)), step)
            results.append(done)
        return results

    def receive_pieces(self, arrived):
        slots = self.receive_rows(arrived, lambda pieces, slot: (pieces, None))
        return [piece for pieces in slots for piece in pieces]

    def send_direct(self, own):
        if not self.paired:
            return self.send_rows(own)
        return [self.across(own, step) if step else own for step in range(4)]

    def direct_pieces(self, arrived):
        if not self.paired:
            return arrived
        return [piece for here in arrived for piece in (here, self.swap(here))]

    def chip_sums(self, pieces):
        if not self.paired:
            return pieces
        return [
            mine + self.swap(other.astype(low)).astype(full)
            for mine, other in zip(pieces[::2], pieces[1::2])
        ]

    def reduce_rows(self, sums, first_fill=None, second_fill=None):
        if not self.paired:
            return lax.psum_scatter(
                sums[0].astype(low), ("ctx", "tp"), scatter_dimension=0, tiled=True
            ).astype(full)
        own, first, second, far = sums
        half = own.shape[0] // 2
        far = far.astype(low)
        early = [
            self.across(far[:half], 1),
            self.across(far[half:], 2),
            self.across(first[:half].astype(low), 1),
            self.across(second[half:].astype(low), 2),
        ]
        if second_fill is not None:
            early[:2], first_fill = tied(early[:2], first_fill)
        far_top, far_end, first_top, second_end = [part.astype(full) for part in early]
        late = [(second[:half] + far_top).astype(low), (first[half:] + far_end).astype(low)]
        if second_fill is not None:
            late, first_fill = tied(late, first_fill)
        late = [self.across(late[0], 2), self.across(late[1], 1)]
        if second_fill is not None:
            fill = second_fill(first_fill)
            late, fill = tied(late, fill)
        second_top, first_end = [part.astype(full) for part in late]
        result = own + jnp.concatenate([first_top + second_top, first_end + second_end], axis=0)
        return result if second_fill is None else (result, fill)

    def send_sums(self, sums):
        if not self.paired:
            return sums
        return [sums[0]] + [self.across(sums[step].astype(low), step) for step in range(1, 4)]

    def add_sums(self, arrived):
        if not self.paired:
            return self.reduce_rows(arrived)
        return sum([part.astype(full) for part in arrived[1:]], arrived[0])

    def both_halves(self, value):
        if not self.paired:
            return lax.all_gather(value, "tp", axis=0, tiled=True)
        other = self.swap(value)
        return jnp.where(
            self.tp == 0,
            jnp.concatenate([value, other], axis=0),
            jnp.concatenate([other, value], axis=0),
        )

    def exchange(self, value, axis, count):
        parts = [value] + [
            lax.ppermute(value, axis, [(i, i ^ step) for i in range(count)])
            for step in range(1, count)
        ]
        while len(parts) > 1:
            parts = [left + right for left, right in zip(parts[::2], parts[1::2])]
        return parts[0]

    def total(self, norms, biases):
        if not self.paired:
            return (lax.psum(norms, ("shard", "ctx", "tp")), lax.psum(biases, ("shard", "ctx")))
        flat = self.exchange(norms.reshape(-1, LANES), "tp", self.tp_count)
        count = flat.shape[0]
        flat = jnp.concatenate([flat, biases.reshape(-1, LANES)], axis=0)
        flat = self.exchange(flat, "ctx", self.ctx_count)
        flat = self.exchange(flat, "shard", self.shard_count)
        return (flat[:count].reshape(norms.shape), flat[count:].reshape(biases.shape))


    def send_heads(self, qkv, out):
        size = out.shape[1] // self.ctx_count
        parts = []
        for step in range(self.ctx_count):
            start = (self.ctx ^ step) * size
            piece = jnp.concatenate(
                [
                    pair_columns(lax.dynamic_slice_in_dim(qkv, start, size, 2)),
                    lax.dynamic_slice_in_dim(out, start, size, 1),
                ],
                axis=1,
            )
            piece = jnp.moveaxis(piece.reshape(LANES, -1, LANES), 1, 0).reshape(-1, LANES)
            parts.append(self.across(piece, step) if step else piece)
        return parts

    def cut_layer(self, heads, gate_up, down):
        arrays = [jnp.moveaxis(gate_up, 1, 0), down]
        rows = 3 * down.shape[1] // self.ctx_count
        if heads is not None:
            qkv, out = heads
            arrays = [jnp.moveaxis(qkv, 1, 0), out] + arrays
            rows += 4 * out.shape[1] // self.ctx_count
        return local_kernel(
            functools.partial(cut_kernel, self.ctx_count, heads is not None),
            self.ctx,
            arrays,
            jax.ShapeDtypeStruct((self.ctx_count, rows, LANES), low),
        )

    def send_cut(self, cut):
        return [self.across(cut[k], k) if k else cut[k] for k in range(self.ctx_count)]

    def join_parts(self, parts, units, columns):
        features = LANES * self.ctx_count
        return local_kernel(
            functools.partial(join_kernel, self.ctx_count, len(units)),
            self.ctx,
            parts,
            [jax.ShapeDtypeStruct((size, features), low) for size in units]
            + [jax.ShapeDtypeStruct((features, size), low) for size in columns],
        )

    def split_send(self, value):
        if not self.paired:
            return [value]
        parts = []
        for step in range(self.ctx_count):
            piece = lax.dynamic_slice_in_dim(value, (self.ctx ^ step) * LANES, LANES, 1)
            parts.append(self.across(piece, step) if step else piece)
        return parts

    def join_units(self, parts, tp_units, layer, layer_total, earlier):
        units = tp_units // self.ctx_count
        if not self.paired:
            gate_up = parts[0][: 2 * units].reshape(2, units, -1)
            gate_up = self.spread(gate_up, 2, 1)
            down = self.spread(parts[0][2 * units : 3 * units], 1, 0)
            values = (jnp.transpose(gate_up, (2, 0, 1)), jnp.transpose(down))
            return self.stack_layer(values, layer, layer_total, earlier)
        return stacked_kernel(
            functools.partial(join_units_kernel, self.ctx_count),
            self.ctx,
            parts,
            layer,
            layer_total,
            [(LANES, 2, tp_units), (LANES, tp_units)],
            earlier,
            [pltpu.VMEM((tp_units, LANES), low)],
        )

    def join_heads(self, parts, width, layer, layer_total, earlier):
        if not self.paired:
            columns = 4 * (-(-width // LANES) * LANES)
            qkv = unpair_columns(parts[0][-columns : -columns // 4].T, width)
            out = parts[0][-columns // 4 :].T[:, :width]
            values = (jnp.swapaxes(self.spread(qkv, 0, 2), 0, 1), self.spread(out, 0, 1))
            return self.stack_layer(values, layer, layer_total, earlier)
        tp_width = width * self.ctx_count
        return stacked_kernel(
            functools.partial(join_heads_kernel, self.ctx_count),
            self.ctx,
            parts,
            layer,
            layer_total,
            [(3, LANES, tp_width), (LANES, tp_width)],
            earlier,
        )


    def stack_layer(self, values, layer, layer_total, earlier):
        if earlier is None:
            earlier = [jnp.zeros((layer_total,) + value.shape, full) for value in values]
        return [stack.at[layer].set(value.astype(full)) for stack, value in zip(earlier, values)]

    def spread(self, value, split_axis, join_axis):
        return lax.all_to_all(value, "ctx", split_axis, join_axis, tiled=True)

    def spread_layer(self, qkv, out, gate_up, down):
        gate_up = self.spread(jnp.transpose(gate_up, (1, 2, 0)), 1, 2)
        return (
            over_shard(pair_columns(self.spread(qkv, 2, 0)), 0),
            over_shard(pad_columns(self.spread(out, 1, 0)), 0),
            over_shard(gate_up.reshape(-1, gate_up.shape[2]), 1),
            over_shard(self.spread(jnp.transpose(down), 0, 1), 1),
        )


def pair_columns(weight):
    width = weight.shape[-1]
    pairs = -(-width // LANES)
    if pairs * LANES != width:
        weight = jnp.pad(weight, [(0, 0)] * (weight.ndim - 1) + [(0, pairs * LANES - width)])
    lead = weight.shape[:-2]
    weight = weight.reshape(lead + (3, pairs, LANES))
    return jnp.moveaxis(weight, -2, -3).reshape(lead + (pairs * 3 * LANES,))


def unpair_columns(value, width):
    lead = value.shape[:-1]
    pairs = value.shape[-1] // (3 * LANES)
    value = jnp.moveaxis(value.reshape(lead + (pairs, 3, LANES)), -3, -2)
    return value.reshape(lead + (3, pairs * LANES))[..., :width]


def pad_columns(weight):
    width = weight.shape[-1]
    filled = -(-width // LANES) * LANES
    return weight if filled == width else jnp.pad(weight, [(0, 0), (0, filled - width)])


def sum_dots(groups):
    return jnp.concatenate([dot_tn(lefts[0], rights[0]) for lefts, rights in groups]).astype(low)


def flat_pieces(slots_done):
    return [[piece for pieces in kind for piece in pieces] for kind in zip(*slots_done)]


def over_shard(value, axis):
    return lax.all_gather(value, "shard", axis=axis, tiled=True)


def sum_shard(value, axis):
    return lax.psum_scatter(value, "shard", scatter_dimension=axis, tiled=True)


def body(
    tokens,
    cotangent,
    lengths,
    norm_gain,
    norm_bias,
    input_bias,
    input_projection,
    output_projection,
    gate_up_weight,
    down_weight,
):
    held_rows = tokens.shape[0]
    layer_total = input_projection.shape[0]
    tp_width = input_bias.shape[2]
    ctx_count, tp_count = lax.axis_size("ctx"), lax.axis_size("tp")
    width = tp_width // ctx_count
    hidden_width = down_weight.shape[2] // ctx_count
    rows = held_rows // tp_count
    group = Group(width, hidden_width, input_projection.shape[1], rows)
    seq_ids, length, offset = row_meta(lengths[0], held_rows)
    positions = (
        jnp.arange(ctx_count, dtype=jnp.int32)[:, None] * length[None, :] + offset[None, :]
    ).reshape(-1)
    lane = jnp.arange(LANES, dtype=jnp.int32)[None, :]
    same = lane == seq_ids[:, None]
    named = lane < lengths.shape[1]
    query_mark = jnp.where(named & ~same, blocked, 0.0).astype(low)
    key_mark = jnp.where(same, 1.0, 0.0).astype(low)
    tables = wide_rotary_tables(positions) + (query_mark, key_mark)
    order = group.order()
    bias_own = lax.dynamic_slice_in_dim(input_bias, group.ctx * width, width, 2)
    bias_pairs = pair_columns(bias_own).reshape(layer_total, -1, 3, LANES)

    def own_rows(value):
        return lax.dynamic_slice_in_dim(value, group.tp * rows, rows, 0)

    def sources(index):
        return (
            input_projection[index],
            output_projection[index],
            gate_up_weight[index],
            down_weight[index],
        )

    def norm_one(index, stream):
        scaled, inverse, normed = norm_parts(stream, norm_gain[index, 0], norm_bias[index, 0])
        return (scaled, inverse, group.send_rows(normed.astype(low)))

    stream = own_rows(tokens).astype(full)
    qkv_columns = 3 * width

    def split_heads(heads_full):
        return (heads_full, heads_full[:, qkv_columns:])

    def split_units(units_full):
        return (
            units_full[:hidden_width],
            units_full[hidden_width : 2 * hidden_width],
            units_full[2 * hidden_width :],
        )

    if group.paired:
        (heads_part,) = group.join_parts(
            group.send_heads(*sources(0)[:2]), [], [qkv_columns + width]
        )
        heads_full = over_shard(heads_part, 0)
        first_norm = norm_one(0, stream)
        cut = tied(group.cut_layer(None, *sources(0)[2:]), first_norm[2])[0]
        (units_part,) = group.join_parts(group.send_cut(cut), [3 * hidden_width], [])
        weights = [split_heads(heads_full) + (over_shard(units_part, 1),)]
    else:
        first_norm = norm_one(0, stream)
        weights = []
        for index in range(layer_total):
            qkv_full, out_full, gate_up_full, down_full = group.spread_layer(*sources(index))
            weights.append(
                (qkv_full, out_full)
                + (jnp.concatenate([gate_up_full, down_full], axis=0),)
            )

    saved = []
    for index in range(layer_total):
        last = index + 1 == layer_total
        qkv_weight, out_weight, units_full = weights[index]
        gate_weight, up_weight, down = split_units(units_full)
        scaled_one, inverse_one, arrived = norm_one(index, stream) if index else first_norm
        normed_one = group.receive_pieces(arrived)
        travel = None
        if last:
            grad_own, normed_one = tied(own_rows(cotangent), normed_one)
            travel = group.send_direct(grad_own)
        elif group.paired:
            travel = group.send_cut(
                tied(
                    group.cut_layer(sources(index + 1)[:2], *sources(index + 1)[2:]), normed_one
                )[0]
            )
        heads, fine, totals, rotated = attend(
            order, normed_one, qkv_weight, bias_pairs[index], tables, ctx_count, tp_count
        )
        if travel is not None:
            heads, travel = tied(heads, travel)
        if group.paired and not last:
            units_part, heads_part = group.join_parts(
                travel, [3 * hidden_width], [qkv_columns + width]
            )
            heads = tied(heads, (units_part, heads_part))[0]
            weights.append(
                split_heads(over_shard(heads_part, 0)) + (over_shard(units_part, 1),)
            )
        attention = group.reduce_rows(
            group.chip_sums([dot_nt(rows_in, out_weight) for rows_in in heads])
        )
        middle = stream + attention
        if last:
            (last_branch, units_full), middle = tied(
                (group.direct_pieces(travel), units_full), middle
            )
            gate_weight, up_weight, down = split_units(units_full)
            weights[index] = (qkv_weight, out_weight, units_full)
        scaled_two, inverse_two, normed_two = norm_parts(
            middle, norm_gain[index, 1], norm_bias[index, 1]
        )

        def forward_units(pieces, slot):
            if group.paired and not last:
                feeds, gates, ups, hidden = units_call(pieces, units_full)
                return ((pieces, gates, ups, hidden, feeds), feeds)
            gates = [dot_nt(rows_in, gate_weight) for rows_in in pieces]
            ups = [dot_nt(rows_in, up_weight) for rows_in in pieces]
            hidden = [(jax.nn.silu(gate) * up).astype(low) for gate, up in zip(gates, ups)]
            feeds = [dot_nn(units, down) for units in hidden if not last]
            return ((pieces, gates, ups, hidden, feeds), hidden)

        arrived = group.send_rows(normed_two.astype(low))
        if last:
            slots_done = group.receive_rows(arrived, forward_units)
            normed_two, gates, ups, hidden, feeds = flat_pieces(slots_done)
        else:
            pieces = lax.optimization_barrier(group.receive_pieces(arrived))
            size = len(pieces) // (4 if group.paired else 1)
            slots_done = [
                forward_units(pieces[i : i + size], i // size)[0]
                for i in range(0, len(pieces), size)
            ]
            normed_two, gates, ups, hidden, feeds = flat_pieces(slots_done)
            feeds = group.chip_sums(feeds)
            stream = middle + group.reduce_rows(feeds)
            if group.paired:
                stream, heads_full = tied(stream, weights[index + 1][0])
                weights[index + 1] = split_heads(heads_full) + weights[index + 1][2:]
        saved.append(
            (
                scaled_one,
                inverse_one,
                normed_one,
                heads,
                fine,
                totals,
                rotated,
                scaled_two,
                inverse_two,
                normed_two,
                gates,
                ups,
                hidden,
            )
        )

    grad_stream = own_rows(cotangent).astype(full)
    norm_list = [None] * layer_total
    input_bias_list = [None] * layer_total
    head_stacks = None
    unit_stacks = None
    waiting = None
    for index in reversed(range(layer_total)):
        last = index + 1 == layer_total
        (
            scaled_one,
            inverse_one,
            normed_one,
            heads,
            fine,
            totals,
            rotated,
            scaled_two,
            inverse_two,
            normed_two,
            gates,
            ups,
            hidden,
        ) = saved[index]
        qkv_weight, out_weight, units_full = weights[index]
        gate_weight, up_weight, down = split_units(units_full)


        def backward_units(pieces, slot):
            grad_gates, grad_ups, partials = [], [], []
            for place, rows_in in enumerate(pieces, slot * len(pieces)):
                gate, up = gates[place], ups[place]
                grad_hidden = dot_nt(rows_in, down)
                sigmoid_gate = jax.nn.sigmoid(gate)
                grad_gates.append(
                    (
                        grad_hidden * up * (sigmoid_gate * (1.0 + gate * (1.0 - sigmoid_gate)))
                    ).astype(low)
                )
                grad_ups.append((grad_hidden * (gate * sigmoid_gate)).astype(low))
                partials.append(
                    dot_nn(grad_gates[-1], gate_weight) + dot_nn(grad_ups[-1], up_weight)
                )
            return ((pieces, grad_gates, grad_ups, partials), (grad_gates, grad_ups))

        if last:
            size = len(last_branch) // (4 if group.paired else 1)
            slots_done = [
                backward_units(last_branch[i : i + size], i // size)[0]
                for i in range(0, len(last_branch), size)
            ]
        else:
            slots_done = group.receive_rows(
                group.send_rows(grad_stream.astype(low)), backward_units
            )
        branch, grad_gates, grad_ups, partials = flat_pieces(slots_done)
        sums = group.chip_sums(partials)
        (branch, grad_gates, grad_ups, hidden), unused = tied(
            (branch, grad_gates, grad_ups, hidden), sums
        )
        if group.paired:
            down_grad = weight_grads([(hidden, branch)], 3 * hidden_width, 2 * hidden_width)
            grad_normed_two, units_grad = group.reduce_rows(
                sums,
                down_grad,
                lambda earlier: weight_grads(
                    [(grad_gates, normed_two), (grad_ups, normed_two)],
                    3 * hidden_width,
                    0,
                    earlier,
                ),
            )
        else:
            units_grad = sum_dots(
                [(grad_gates, normed_two), (grad_ups, normed_two), (hidden, branch)]
            )
            grad_normed_two = group.reduce_rows(sums)
        units_part = sum_shard(units_grad, 1)
        if last:
            feeds = group.chip_sums([dot_nn(units, down) for units in hidden])
        grad_input_two, gain_two, bias_two = norm_back(
            grad_normed_two, scaled_two, inverse_two, norm_gain[index, 1]
        )
        grad_middle = grad_stream + grad_input_two
        branch = group.receive_pieces(group.send_rows(grad_middle.astype(low)))
        grad_heads = [dot_nn(rows_in, out_weight).astype(low) for rows_in in branch]
        if last:
            travel = group.send_sums(tied(feeds, grad_heads)[0])
        else:
            travel = group.split_send(tied(waiting, grad_heads)[0])
        grad_qkv, bias_sums = attend_back(
            order, rotated, grad_heads, fine, totals, tables, ctx_count, tp_count
        )
        grad_qkv, travel, branch = lax.optimization_barrier((grad_qkv, travel, branch))
        if last:
            result = (middle + group.add_sums(travel)).astype(low)
        else:
            unit_stacks = group.join_units(
                travel, hidden_width * ctx_count, index + 1, layer_total, unit_stacks
            )
            head_stacks = group.join_heads(travel, width, index + 1, layer_total, head_stacks)
        sums = group.chip_sums(
            [dot_nt(rows_in, qkv_weight[:, : rows_in.shape[1]]) for rows_in in grad_qkv]
        )
        if group.paired:
            grad_normed_one, heads_grad = group.reduce_rows(
                sums,
                (grad_qkv, branch),
                lambda held: weight_grads([(held[0], normed_one), (heads, held[1])]),
            )
        else:
            heads_grad = sum_dots([(grad_qkv, normed_one), (heads, branch)])
            grad_normed_one = group.reduce_rows(sums)
        grad_normed_one = tied(grad_normed_one, units_part)[0]
        heads_part = sum_shard(heads_grad, 1)
        if index:
            waiting = jnp.concatenate([units_part, heads_part], axis=0)
        bias_sums = bias_sums[:, :3, :].transpose(1, 0, 2).reshape(3, -1)[:, :width]
        input_bias_list[index] = lax.dynamic_update_slice_in_dim(
            jnp.zeros((3, tp_width), full), bias_sums, group.ctx * width, 1
        )
        grad_input_one, gain_one, bias_one = norm_back(
            grad_normed_one, scaled_one, inverse_one, norm_gain[index, 0]
        )
        grad_stream = grad_middle + grad_input_one
        norm_list[index] = jnp.stack([gain_one, gain_two, bias_one, bias_two])
    unit_stacks = group.join_units(
        group.split_send(units_part), hidden_width * ctx_count, 0, layer_total, unit_stacks
    )
    norm_total, bias_total = group.total(jnp.stack(norm_list), jnp.stack(input_bias_list))
    result = group.both_halves(result)
    tokens_grad = group.both_halves(grad_stream)
    heads_part = tied(heads_part, (unit_stacks, norm_total, bias_total, result, tokens_grad))[0]
    head_stacks = group.join_heads(
        group.split_send(heads_part), width, 0, layer_total, head_stacks
    )
    return (
        result,
        tokens_grad,
        norm_total[:, :2],
        norm_total[:, 2:],
        bias_total,
        jnp.moveaxis(head_stacks[0], 1, 2),
        head_stacks[1],
        unit_stacks[0],
        unit_stacks[1],
    )


def solution(mesh):
    in_specs = (
        P(("shard", "ctx"), None),
        P(("shard", "ctx"), None),
        P("shard", None),
        P(),
        P(),
        P(None, None, "tp"),
        P(None, ("shard", "ctx"), None, "tp"),
        P(None, ("shard", "ctx"), "tp"),
        P(None, ("shard", "ctx"), None, "tp"),
        P(None, ("shard", "ctx"), "tp"),
    )
    out_specs = (
        P(("shard", "ctx"), None),
        P(("shard", "ctx"), None),
        P(),
        P(),
        P(None, None, "tp"),
        P(None, ("shard", "ctx"), None, "tp"),
        P(None, ("shard", "ctx"), "tp"),
        P(None, ("shard", "ctx"), None, "tp"),
        P(None, ("shard", "ctx"), "tp"),
    )
    return jax.shard_map(body, mesh=mesh, in_specs=in_specs, out_specs=out_specs, check_vma=False)
```

```python
import functools
import math

import jax
import jax.numpy as jnp
from jax import lax
from jax.experimental import pallas as pl
from jax.experimental.pallas import tpu as pltpu
from jax.sharding import PartitionSpec as P

HEAD = 64
ROT = 16
LANES = 128

norm_eps = 1e-05
rotary_base = 10000.0
blocked = -(2.0**100)
low = jnp.bfloat16
full = jnp.float32


def row_meta(seq_lengths, row_count):
    seq_ends = jnp.cumsum(seq_lengths, dtype=jnp.int32)
    row_index = jnp.arange(row_count, dtype=jnp.int32)
    seq_ids = jnp.sum(
        (row_index[:, None] >= seq_ends[None, :]).astype(jnp.int32), axis=1, dtype=jnp.int32
    )
    one_hot = (
        seq_ids[:, None] == jnp.arange(seq_lengths.shape[0], dtype=jnp.int32)[None, :]
    ).astype(jnp.int32)
    seq_start = jnp.sum(one_hot * (seq_ends - seq_lengths)[None, :], axis=1, dtype=jnp.int32)
    length = jnp.sum(one_hot * seq_lengths[None, :], axis=1, dtype=jnp.int32)
    return (seq_ids, length, row_index - seq_start)


def wide_rotary_tables(positions):
    half_rot = ROT // 2
    frequency = rotary_base ** (-(2.0 * jnp.arange(half_rot, dtype=full)) / ROT)
    lane = jnp.arange(LANES, dtype=jnp.int32) % HEAD
    lane_frequency = jnp.where(lane < ROT, jnp.tile(frequency, LANES // half_rot), 0.0)
    sign = jnp.where(lane < half_rot, -1.0, 1.0)
    angles = positions.astype(full)[:, None] * lane_frequency[None, :]
    return (jnp.cos(angles), jnp.sin(angles) * sign[None, :])


def norm_parts(stream, gain_row, bias_row):
    row_mean = jnp.mean(stream, axis=-1, keepdims=True)
    centered = stream - row_mean
    variance = jnp.mean(centered * centered, axis=-1, keepdims=True)
    inverse = lax.rsqrt(variance + norm_eps)
    scaled = centered * inverse
    return (scaled, inverse, scaled * gain_row + bias_row)


def norm_back(grad_normed, scaled, inverse, gain_row):
    grad_scaled = grad_normed * gain_row
    inner = (
        grad_scaled
        - jnp.mean(grad_scaled, axis=-1, keepdims=True)
        - scaled * jnp.mean(grad_scaled * scaled, axis=-1, keepdims=True)
    )
    return (inverse * inner, jnp.sum(grad_normed * scaled, axis=0), jnp.sum(grad_normed, axis=0))


def dot_nn(left, right):
    return lax.dot_general(left, right, (((1,), (0,)), ((), ())), preferred_element_type=full)


def dot_nt(left, right):
    return lax.dot_general(left, right, (((1,), (1,)), ((), ())), preferred_element_type=full)


def dot_tn(left, right):
    return lax.dot_general(left, right, (((0,), (0,)), ((), ())), preferred_element_type=full)


def partner(values, lane):
    near = pltpu.roll(values, LANES - ROT // 2, 1)
    far = pltpu.roll(values, ROT // 2, 1)
    return jnp.where(lane % HEAD < ROT // 2, near, far)


def attend_kernel(ctx_count, tp_count, slots, order_ref, *refs):
    normed_refs = refs[:slots]
    weight_ref, bias_ref, cos_ref, sin_ref, query_mark_ref, key_mark_ref = refs[slots : slots + 6]
    out_refs = refs[slots + 6 : 2 * slots + 6]
    fine_ref, total_ref, rotated_ref, key_wide = refs[2 * slots + 6 :]
    rows_all = rotated_ref.shape[0]
    block = rows_all // ctx_count
    part = block // tp_count
    slot_parts = ctx_count * tp_count // slots
    lane_part = lax.broadcasted_iota(jnp.int32, (part, LANES), 1)
    to_exponent = float(HEAD) ** (-0.5) * math.log2(math.e)

    for place in range(ctx_count * tp_count):
        slot, start = place // slot_parts, place % slot_parts * part
        source = slice(start, start + part)
        target = pl.ds(pl.multiple_of(order_ref[place] * part, part), part)
        mark = pl.ds(pl.multiple_of(lax.rem(order_ref[place], tp_count) * part, part), part)
        cosine = cos_ref[target, :]
        sine = sin_ref[target, :]
        joined = dot_nn(normed_refs[slot][source, :], weight_ref[...])
        for kind in range(3):
            columns = slice(kind * LANES, (kind + 1) * LANES)
            values = joined[:, columns] + bias_ref[0, kind : kind + 1, :]
            if kind < 2:
                values = values * cosine + partner(values, lane_part) * sine
            rotated_ref[target, columns] = values.astype(low)
        key_wide[target, :LANES] = rotated_ref[target, LANES : 2 * LANES]
        key_wide[target, LANES:] = key_mark_ref[mark, :]

    tile = min(256, block)
    lane_tile = lax.broadcasted_iota(jnp.int32, (tile, LANES), 1)
    row_index = lax.broadcasted_iota(jnp.int32, (tile, block), 0)
    column_index = lax.broadcasted_iota(jnp.int32, (tile, block), 1)
    for place in range(ctx_count):
        past = place * block
        for head in range(2):

            def step(sub, unused):
                start = pl.multiple_of(sub * tile, tile)
                rows = pl.ds(pl.multiple_of(past + sub * tile, tile), tile)
                own_lanes = lane_tile // HEAD == head
                query = rotated_ref[rows, :LANES]
                query = jnp.concatenate(
                    [
                        jnp.where(own_lanes, query, jnp.zeros_like(query)),
                        query_mark_ref[pl.ds(start, tile), :],
                    ],
                    axis=1,
                )
                near = dot_nt(query, key_wide[past : past + block, :])
                near = jnp.where(column_index <= row_index + start, near, blocked)
                top = jnp.max(near, axis=1, keepdims=True)
                if past:
                    far = dot_nt(query, key_wide[:past, :])
                    top = jnp.maximum(top, jnp.max(far, axis=1, keepdims=True))
                shift = top * to_exponent
                near = jnp.exp2(near * to_exponent - shift)
                total = jnp.sum(near, axis=1, keepdims=True)
                out = dot_nn(near.astype(low), rotated_ref[past : past + block, 2 * LANES :])
                if past:
                    far = jnp.exp2(far * to_exponent - shift)
                    total = total + jnp.sum(far, axis=1, keepdims=True)
                    out = out + dot_nn(far.astype(low), rotated_ref[:past, 2 * LANES :])
                out = out / total
                fine_ref[rows, :] = jnp.where(own_lanes, out, fine_ref[rows, :])
                log_total = jnp.broadcast_to(shift + jnp.log2(total), (tile, LANES))
                total_ref[0, head : head + 1, rows] = jnp.transpose(log_total)[:1, :]
                return unused

            lax.fori_loop(0, block // tile, step, 0)

    for place in range(ctx_count * tp_count):
        slot, start = place // slot_parts, place % slot_parts * part
        source = pl.ds(pl.multiple_of(order_ref[place] * part, part), part)
        out_refs[slot][start : start + part, :] = fine_ref[source, :].astype(low)


def attend_back_kernel(ctx_count, tp_count, slots, order_ref, rotated_ref, *refs):
    grad_refs = refs[:slots]
    fine_ref, total_ref, cos_ref, sin_ref, query_mark_ref, key_mark_ref = refs[slots : slots + 6]
    out_refs = refs[slots + 6 : 2 * slots + 6]
    (
        sum_ref,
        query_wide,
        key_wide,
        key_turned,
        grad_own,
        row_dots,
        grad_query,
        grad_key,
        grad_value,
        query_rows_grad,
    ) = refs[2 * slots + 6 :]
    rows_all = rotated_ref.shape[0]
    slot_parts = ctx_count * tp_count // slots
    block = rows_all // ctx_count
    part = block // tp_count
    score_scale = float(HEAD) ** (-0.5)
    to_exponent = score_scale * math.log2(math.e)
    lane_block = lax.broadcasted_iota(jnp.int32, (block, LANES), 1)
    lane_part = lax.broadcasted_iota(jnp.int32, (part, LANES), 1)
    head_row = lax.broadcasted_iota(jnp.int32, (LANES, block), 0)

    for place in range(ctx_count * tp_count):
        slot, start = place // slot_parts, place % slot_parts * part
        target = pl.ds(pl.multiple_of(order_ref[place] * part, part), part)
        grad_own[0, target, :] = grad_refs[slot][start : start + part, :]

    def prepare(place, unused):
        rows = pl.ds(pl.multiple_of(place * block, block), block)
        grad = grad_own[0, rows, :]
        product = jnp.transpose(grad.astype(full) * fine_ref[rows, :])
        turned = jnp.transpose(rotated_ref[rows, LANES : 2 * LANES].astype(full))
        query = rotated_ref[rows, :LANES]
        for head in range(2):
            own_lanes = lane_block // HEAD == head
            row_dots[head : head + 1, rows] = jnp.sum(
                product[head * HEAD : (head + 1) * HEAD, :], axis=0, keepdims=True
            )
            key_turned[head, :, rows] = jnp.where(head_row // HEAD == head, turned, 0.0).astype(low)
            query_wide[head, rows, :LANES] = jnp.where(own_lanes, query, jnp.zeros_like(query))
            query_wide[head, rows, LANES:] = query_mark_ref[...]
            grad_own[head, rows, :] = jnp.where(own_lanes, grad, jnp.zeros_like(grad))
        key_wide[rows, :LANES] = rotated_ref[rows, LANES : 2 * LANES]
        key_wide[rows, LANES:] = key_mark_ref[...]
        grad_query[:, rows] = jnp.zeros((LANES, block), full)
        grad_key[rows, :] = jnp.zeros((block, LANES), full)
        grad_value[rows, :] = jnp.zeros((block, LANES), full)
        return unused

    lax.fori_loop(0, ctx_count, prepare, 0)

    key_index = lax.broadcasted_iota(jnp.int32, (block, block), 0)
    query_index = lax.broadcasted_iota(jnp.int32, (block, block), 1)

    def pair(head, key_rows, query_rows, diagonal):
        query = query_wide[head, query_rows, :]
        scores = dot_nt(key_wide[key_rows, :], query)
        if diagonal:
            scores = jnp.where(key_index <= query_index, scores, blocked)
        probs = jnp.exp2(scores * to_exponent - total_ref[0, head : head + 1, query_rows])
        grad = grad_own[head, query_rows, :]
        grad_probs = dot_nt(rotated_ref[key_rows, 2 * LANES :], grad)
        grad_scores = (probs * (grad_probs - row_dots[head : head + 1, query_rows])).astype(low)
        grad_value[key_rows, :] += dot_nn(probs.astype(low), grad)
        grad_key[key_rows, :] += dot_nn(grad_scores, query[:, :LANES])
        grad_query[:, query_rows] += dot_nn(key_turned[head, :, key_rows], grad_scores)

    for head in range(2):

        def over_keys(key_place, unused, head=head):
            key_rows = pl.ds(pl.multiple_of(key_place * block, block), block)
            pair(head, key_rows, key_rows, True)

            def over_queries(query_place, inner):
                pair(head, key_rows, pl.ds(pl.multiple_of(query_place * block, block), block), False)
                return inner

            return lax.fori_loop(key_place + 1, ctx_count, over_queries, unused)

        lax.fori_loop(0, ctx_count, over_keys, 0)

    sum_ref[...] = jnp.zeros_like(sum_ref)

    def turn(place, unused):
        rows = pl.ds(pl.multiple_of(place * block, block), block)
        query_rows_grad[rows, :] = jnp.transpose(grad_query[:, rows])
        return unused

    lax.fori_loop(0, ctx_count, turn, 0)

    for place in range(ctx_count * tp_count):
        slot, start = place // slot_parts, place % slot_parts * part
        source = pl.ds(pl.multiple_of(order_ref[place] * part, part), part)
        cosine = cos_ref[source, :]
        sine = sin_ref[source, :]
        values = (
            query_rows_grad[source, :] * score_scale,
            grad_key[source, :] * score_scale,
            grad_value[source, :],
        )
        for kind in range(3):
            value = values[kind]
            if kind < 2:
                value = value * cosine - partner(value, lane_part) * sine
            value = value.astype(low)
            out_refs[slot][start : start + part, kind * LANES : (kind + 1) * LANES] = value
            sum_ref[0, kind : kind + 1, :] += jnp.sum(value.astype(full), axis=0, keepdims=True)


def whole(shape):
    return pl.BlockSpec(shape, lambda pair: (0,) * len(shape))


def attend(order, normed, weight, bias, tables, ctx_count, tp_count):
    slots = len(normed)
    slot_rows, features = normed[0].shape
    rows = slots * slot_rows
    pairs = bias.shape[0]
    width = pairs * 3 * LANES
    trio = pl.BlockSpec((rows, 3 * LANES), lambda pair: (0, pair))
    single = pl.BlockSpec((rows, LANES), lambda pair: (0, pair))
    slot_single = pl.BlockSpec((slot_rows, LANES), lambda pair: (0, pair))
    results = pl.pallas_call(
        functools.partial(attend_kernel, ctx_count, tp_count, slots),
        grid=(pairs,),
        in_specs=[pl.BlockSpec(memory_space=pltpu.SMEM)]
        + [whole((slot_rows, features))] * slots
        + [pl.BlockSpec((features, 3 * LANES), lambda pair: (0, pair))]
        + [pl.BlockSpec((1, 3, LANES), lambda pair: (pair, 0, 0))]
        + [whole(table.shape) for table in tables],
        out_specs=[slot_single] * slots
        + [
            single,
            pl.BlockSpec((1, 8, rows), lambda pair: (pair, 0, 0)),
            trio,
        ],
        out_shape=[jax.ShapeDtypeStruct((slot_rows, pairs * LANES), low)] * slots
        + [
            jax.ShapeDtypeStruct((rows, pairs * LANES), full),
            jax.ShapeDtypeStruct((pairs, 8, rows), full),
            jax.ShapeDtypeStruct((rows, width), low),
        ],
        scratch_shapes=[pltpu.VMEM((rows, 2 * LANES), low)],
        compiler_params=pltpu.CompilerParams(vmem_limit_bytes=52 * 2**20),
        cost_estimate=pl.CostEstimate(
            flops=pairs * rows * rows * LANES * 32, bytes_accessed=0, transcendentals=0
        ),
        name="attend",
    )(order, *normed, weight, bias, *tables)
    return (results[:slots], *results[slots:])


def attend_back(order, rotated, grads, fine, totals, tables, ctx_count, tp_count):
    slots = len(grads)
    rows, width = rotated.shape
    slot_rows = rows // slots
    pairs = width // (3 * LANES)
    trio = pl.BlockSpec((rows, 3 * LANES), lambda pair: (0, pair))
    single = pl.BlockSpec((rows, LANES), lambda pair: (0, pair))
    slot_trio = pl.BlockSpec((slot_rows, 3 * LANES), lambda pair: (0, pair))
    slot_single = pl.BlockSpec((slot_rows, LANES), lambda pair: (0, pair))
    results = pl.pallas_call(
        functools.partial(attend_back_kernel, ctx_count, tp_count, slots),
        grid=(pairs,),
        in_specs=[pl.BlockSpec(memory_space=pltpu.SMEM), trio]
        + [slot_single] * slots
        + [single, pl.BlockSpec((1, 8, rows), lambda pair: (pair, 0, 0))]
        + [whole(table.shape) for table in tables],
        out_specs=[slot_trio] * slots + [pl.BlockSpec((1, 8, LANES), lambda pair: (pair, 0, 0))],
        out_shape=[jax.ShapeDtypeStruct((slot_rows, width), low)] * slots
        + [jax.ShapeDtypeStruct((pairs, 8, LANES), full)],
        scratch_shapes=[
            pltpu.VMEM((2, rows, 2 * LANES), low),
            pltpu.VMEM((rows, 2 * LANES), low),
            pltpu.VMEM((2, LANES, rows), low),
            pltpu.VMEM((2, rows, LANES), low),
            pltpu.VMEM((8, rows), full),
            pltpu.VMEM((LANES, rows), full),
            pltpu.VMEM((rows, LANES), full),
            pltpu.VMEM((rows, LANES), full),
            pltpu.VMEM((rows, LANES), full),
        ],
        compiler_params=pltpu.CompilerParams(vmem_limit_bytes=52 * 2**20),
        cost_estimate=pl.CostEstimate(
            flops=pairs * rows * rows * LANES * 32, bytes_accessed=0, transcendentals=0
        ),
        name="attend_back",
    )(order, rotated, *grads, fine, totals, *tables)
    return (results[:slots], results[slots])


def cut_kernel(ctx_count, with_heads, ctx_ref, *refs):
    gate_up_ref, down_ref, sent_ref = refs[-3:]
    units = down_ref.shape[1] // ctx_count
    for kind in range(3):
        weight = down_ref[...] if kind == 2 else gate_up_ref[kind]
        turned = jnp.transpose(weight.astype(full)).astype(low)
        for place in range(ctx_count):
            sent_ref[ctx_ref[0] ^ place, kind * units : (kind + 1) * units, :] = turned[
                place * units : (place + 1) * units
            ]
    if not with_heads:
        return
    qkv_ref, out_weight_ref = refs[:2]
    width = out_weight_ref.shape[1] // ctx_count
    for place in range(ctx_count):
        start = 3 * units
        for kinds in (range(3), (None,)):
            for pair in range(width // LANES):
                columns = slice(place * width + pair * LANES, place * width + (pair + 1) * LANES)
                for kind in kinds:
                    tile = (
                        out_weight_ref[:, columns] if kind is None else qkv_ref[kind, :, columns]
                    )
                    sent_ref[ctx_ref[0] ^ place, start : start + LANES, :] = tile
                    start += LANES


def join_kernel(ctx_count, unit_outs, ctx_ref, *refs):
    parts, outs = refs[:ctx_count], refs[ctx_count:]
    for step in range(ctx_count):
        place = pl.ds(pl.multiple_of((ctx_ref[0] ^ step) * LANES, LANES), LANES)
        start = 0
        for out in outs[:unit_outs]:
            out[:, place] = parts[step][start : start + out.shape[0], :]
            start += out.shape[0]
        for out in outs[unit_outs:]:
            for tile in range(out.shape[1] // LANES):
                out[place, tile * LANES : (tile + 1) * LANES] = parts[step][
                    start : start + LANES, :
                ]
                start += LANES


def join_units_kernel(ctx_count, ctx_ref, *refs):
    parts, (gate_up_ref, down_ref, held) = refs[:ctx_count], refs[-3:]
    units = down_ref.shape[2] // ctx_count
    for kind in range(3):
        for step in range(ctx_count):
            rows = pl.ds(pl.multiple_of((ctx_ref[0] ^ step) * units, 16), units)
            held[rows, :] = parts[step][kind * units : (kind + 1) * units, :]
        turned = jnp.transpose(held[...].astype(full))
        if kind == 2:
            down_ref[0] = turned
        else:
            gate_up_ref[0, :, kind, :] = turned


def join_heads_kernel(ctx_count, ctx_ref, *refs):
    parts, (qkv_ref, out_ref) = refs[:ctx_count], refs[-2:]
    width = out_ref.shape[2] // ctx_count
    for step in range(ctx_count):
        place = (ctx_ref[0] ^ step) * width
        start = parts[step].shape[0] - 4 * width
        for kinds in (range(3), (None,)):
            for pair in range(width // LANES):
                columns = pl.ds(pl.multiple_of(place + pair * LANES, LANES), LANES)
                for kind in kinds:
                    tile = jnp.transpose(parts[step][start : start + LANES, :].astype(full))
                    if kind is None:
                        out_ref[0, :, columns] = tile
                    else:
                        qkv_ref[0, kind, :, columns] = tile
                    start += LANES


def weight_grad_kernel(piece_counts, *refs):
    count = sum(piece_counts)
    lefts, rights, (out_ref, turned_ref) = refs[:count], refs[count : 2 * count], refs[2 * count :]
    rows = lefts[0].shape[0]

    @pl.when(pl.program_id(0) == 0)
    def turn():
        start = first = 0
        for pieces in piece_counts:
            width = lefts[first].shape[1]
            for piece in range(pieces):
                turned = jnp.transpose(lefts[first + piece][...].astype(full)).astype(low)
                turned_ref[start : start + width, piece * rows : (piece + 1) * rows] = turned
            first += pieces
            start += width

    start = first = 0
    for pieces in piece_counts:
        width = lefts[first].shape[1]
        total = None
        for piece in range(pieces):
            product = dot_nn(
                turned_ref[start : start + width, piece * rows : (piece + 1) * rows],
                rights[first + piece][...],
            )
            total = product if total is None else total + product
        out_ref[start : start + width, :] = total.astype(low)
        first += pieces
        start += width


def weight_grads(groups, columns_all=None, start=0, earlier=None):
    lefts = [left for group_lefts, unused in groups for left in group_lefts]
    rights = [right for unused, group_rights in groups for right in group_rights]
    columns = sum(group_lefts[0].shape[1] for group_lefts, unused in groups)
    rows, features = rights[0].shape
    pieces = [len(group_lefts) for group_lefts, unused in groups]
    block = 512
    kept = [] if earlier is None else [earlier]

    def kernel(*refs):
        weight_grad_kernel(pieces, *refs[: 2 * sum(pieces)], *refs[-2:])

    return pl.pallas_call(
        kernel,
        grid=(features // block,),
        in_specs=[pl.BlockSpec(left.shape, lambda i: (0, 0)) for left in lefts]
        + [pl.BlockSpec((rows, block), lambda i: (0, i)) for right in rights]
        + [pl.BlockSpec(memory_space=pl.ANY)] * len(kept),
        out_specs=pl.BlockSpec((columns, block), lambda i: (start // columns, i)),
        out_shape=jax.ShapeDtypeStruct((columns_all or columns, features), low),
        input_output_aliases={2 * sum(pieces): 0} if kept else {},
        scratch_shapes=[pltpu.VMEM((columns, max(pieces) * rows), low)],
        compiler_params=pltpu.CompilerParams(vmem_limit_bytes=56 * 2**20),
        cost_estimate=pl.CostEstimate(
            flops=2 * columns * features * max(pieces) * rows,
            bytes_accessed=columns * features * 4,
            transcendentals=0,
        ),
        name="weight_grads",
    )(*lefts, *rights, *kept)


def start_weights(weights_hbm, held_refs, sems):
    units = held_refs[0].shape[0]
    copies = [
        pltpu.make_async_copy(weights_hbm.at[i * units : (i + 1) * units, :], held, sems.at[i])
        for i, held in enumerate(held_refs)
    ]
    for copy in copies:
        copy.start()
    return copies


def units_kernel(
    mine_in,
    other_in,
    weights_hbm,
    mine_out,
    other_out,
    mine_gate,
    other_gate,
    mine_up,
    other_up,
    mine_units,
    other_units,
    gate_w,
    up_w,
    down_w,
    sems,
):
    copies = start_weights(weights_hbm, (gate_w, up_w, down_w), sems)
    work = (
        (other_in, other_out, other_gate, other_up, other_units),
        (mine_in, mine_out, mine_gate, mine_up, mine_units),
    )
    for place, (rows_in, out, gate_out, up_out, units_out) in enumerate(work):
        if place == 0:
            copies[0].wait()
        gate = dot_nt(rows_in[...], gate_w[...])
        gate_out[...] = gate.astype(low)
        if place == 0:
            copies[1].wait()
        up = dot_nt(rows_in[...], up_w[...])
        up_out[...] = up.astype(low)
        units = (gate / (1.0 + jnp.exp(-gate)) * up).astype(low)
        units_out[...] = units
        if place == 0:
            copies[2].wait()
        out[...] = dot_nn(units, down_w[...]).astype(out.dtype)


def units_call(pieces, weights):
    rows, features = pieces[0].shape
    units = weights.shape[0] // 3
    inside = pl.BlockSpec(memory_space=pltpu.VMEM)
    out_shape = (
        [jax.ShapeDtypeStruct((rows, features), kind) for kind in (full, low)]
        + [jax.ShapeDtypeStruct((rows, units), low)] * 4
        + [jax.ShapeDtypeStruct((rows, units), low)] * 2
    )
    done = pl.pallas_call(
        units_kernel,
        in_specs=[inside] * 2 + [pl.BlockSpec(memory_space=pl.ANY)],
        out_specs=[inside] * len(out_shape),
        out_shape=out_shape,
        scratch_shapes=[pltpu.VMEM((units, features), low)] * 3 + [pltpu.SemaphoreType.DMA((3,))],
        compiler_params=pltpu.CompilerParams(vmem_limit_bytes=58 * 2**20),
        cost_estimate=pl.CostEstimate(flops=0, bytes_accessed=0, transcendentals=0),
        name="units",
    )(*pieces, weights)
    return (done[:2], done[2:4], done[4:6], done[6:8])


def halves_kernel(tp_ref, own_ref, other_ref, out_ref):
    rows = own_ref.shape[0]
    for place, ref in ((tp_ref[0], own_ref), (1 - tp_ref[0], other_ref)):
        out_ref[pl.ds(pl.multiple_of(place * rows, rows), rows), :] = ref[...]


def local_kernel(kernel, ctx, arrays, out_shape):
    inside = pl.BlockSpec(memory_space=pltpu.VMEM)
    return pl.pallas_call(
        kernel,
        in_specs=[pl.BlockSpec(memory_space=pltpu.SMEM)] + [inside] * len(arrays),
        out_specs=jax.tree.map(lambda unused: inside, out_shape),
        out_shape=out_shape,
        compiler_params=pltpu.CompilerParams(vmem_limit_bytes=40 * 2**20),
        cost_estimate=pl.CostEstimate(flops=0, bytes_accessed=0, transcendentals=0),
    )(ctx.reshape(1).astype(jnp.int32), *arrays)


def stacked_kernel(kernel, ctx, arrays, layer, layer_total, shapes, earlier, scratch=()):
    inside = pl.BlockSpec(memory_space=pltpu.VMEM)
    earlier = [] if earlier is None else list(earlier)
    return pl.pallas_call(
        kernel,
        grid=(1,),
        in_specs=[pl.BlockSpec(memory_space=pltpu.SMEM)]
        + [inside] * len(arrays)
        + [pl.BlockSpec(memory_space=pl.ANY)] * len(earlier),
        out_specs=[
            pl.BlockSpec((1,) + shape, lambda i, rank=len(shape): (layer,) + (0,) * rank)
            for shape in shapes
        ],
        out_shape=[jax.ShapeDtypeStruct((layer_total,) + shape, full) for shape in shapes],
        input_output_aliases={1 + len(arrays) + i: i for i in range(len(earlier))},
        scratch_shapes=list(scratch),
        compiler_params=pltpu.CompilerParams(vmem_limit_bytes=40 * 2**20),
        cost_estimate=pl.CostEstimate(flops=0, bytes_accessed=0, transcendentals=0),
    )(ctx.reshape(1).astype(jnp.int32), *arrays, *earlier)


def tied(first, second):
    return lax.optimization_barrier((first, second))


class Group:
    def __init__(self, width, hidden_width, depth, rows):
        self.ctx_count = lax.axis_size("ctx")
        self.tp_count = lax.axis_size("tp")
        self.shard_count = lax.axis_size("shard")
        self.ctx = lax.axis_index("ctx")
        self.tp = lax.axis_index("tp")
        self.paired = (
            self.ctx_count == 4
            and self.shard_count in (2, 4)
            and self.tp_count == 2
            and width % LANES == 0
            and hidden_width % 16 == 0
            and depth == LANES
            and rows % 32 == 0
        )

    def order(self):
        places = jnp.arange(self.ctx_count * self.tp_count, dtype=jnp.int32)
        if not self.paired:
            return places
        away = (places // self.tp_count) ^ self.ctx
        return away * self.tp_count + ((places % self.tp_count) ^ self.tp)

    def across(self, value, step):
        return lax.ppermute(value, "ctx", [(i, i ^ step) for i in range(self.ctx_count)])

    def swap(self, value):
        return lax.ppermute(value, "tp", [(0, 1), (1, 0)])

    def send_rows(self, own):
        if not self.paired:
            return [lax.all_gather(own, ("ctx", "tp"), axis=0, tiled=True)]
        return [own, self.across(own, 1), self.across(own, 2)]

    def receive_rows(self, arrived, work):
        if not self.paired:
            return [work((arrived[0],), 0)[0]]
        own, first, second = arrived
        half = own.shape[0] // 2
        far_top = self.across(first[:half], 2)
        far_end = self.across(second[half:], 1)
        results = []
        behind = None
        for step in range(4):
            here = (own, first, second, None)[step]
            if step == 3:
                here = jnp.concatenate([far_top, far_end], axis=0)
            if behind is not None:
                here = tied(here, behind)[0]
            done, behind = work((here, self.swap(here)), step)
            results.append(done)
        return results

    def receive_pieces(self, arrived):
        slots = self.receive_rows(arrived, lambda pieces, slot: (pieces, None))
        return [piece for pieces in slots for piece in pieces]

    def send_direct(self, own):
        if not self.paired:
            return self.send_rows(own)
        return [self.across(own, step) if step else own for step in range(4)]

    def direct_pieces(self, arrived):
        if not self.paired:
            return arrived
        return [piece for here in arrived for piece in (here, self.swap(here))]

    def chip_sums(self, pieces):
        if not self.paired:
            return pieces
        return [
            mine + self.swap(other.astype(low)).astype(full)
            for mine, other in zip(pieces[::2], pieces[1::2])
        ]

    def reduce_rows(self, sums, first_fill=None, second_fill=None, at_once=False):
        if not self.paired:
            return lax.psum_scatter(
                sums[0].astype(low), ("ctx", "tp"), scatter_dimension=0, tiled=True
            ).astype(full)
        own, first, second, far = sums
        half = own.shape[0] // 2
        far = far.astype(low)
        early = [far[:half], far[half:], first[:half].astype(low), second[half:].astype(low)]
        if at_once:
            early, first_fill = tied(early, first_fill)
            fill = second_fill(first_fill)
        early = [self.across(part, 1 + place % 2) for place, part in enumerate(early)]
        if second_fill is not None and not at_once:
            early[:2], first_fill = tied(early[:2], first_fill)
        far_top, far_end, first_top, second_end = [part.astype(full) for part in early]
        late = [(second[:half] + far_top).astype(low), (first[half:] + far_end).astype(low)]
        if at_once:
            late, fill = tied(late, fill)
        elif second_fill is not None:
            late, first_fill = tied(late, first_fill)
        late = [self.across(late[0], 2), self.across(late[1], 1)]
        if second_fill is not None and not at_once:
            fill = second_fill(first_fill)
            late, fill = tied(late, fill)
        second_top, first_end = [part.astype(full) for part in late]
        result = own + jnp.concatenate([first_top + second_top, first_end + second_end], axis=0)
        return result if second_fill is None else (result, fill)

    def send_sums(self, sums):
        if not self.paired:
            return sums
        return [sums[0]] + [self.across(sums[step].astype(low), step) for step in range(1, 4)]

    def add_sums(self, arrived):
        if not self.paired:
            return self.reduce_rows(arrived)
        return sum([part.astype(full) for part in arrived[1:]], arrived[0])

    def both_halves(self, value):
        if not self.paired:
            return lax.all_gather(value, "tp", axis=0, tiled=True)
        rows, columns = value.shape
        return local_kernel(
            halves_kernel,
            self.tp,
            [value, self.swap(value)],
            jax.ShapeDtypeStruct((self.tp_count * rows, columns), value.dtype),
        )

    def exchange(self, value, axis, count):
        parts = [value] + [
            lax.ppermute(value, axis, [(i, i ^ step) for i in range(count)])
            for step in range(1, count)
        ]
        while len(parts) > 1:
            parts = [left + right for left, right in zip(parts[::2], parts[1::2])]
        return parts[0]

    def total(self, norms, biases):
        if not self.paired:
            return (lax.psum(norms, ("shard", "ctx", "tp")), lax.psum(biases, ("shard", "ctx")))
        flat = self.exchange(norms.reshape(-1, LANES), "tp", self.tp_count)
        count = flat.shape[0]
        flat = jnp.concatenate([flat, biases.reshape(-1, LANES)], axis=0)
        flat = self.exchange(flat, "ctx", self.ctx_count)
        flat = self.exchange(flat, "shard", self.shard_count)
        return (flat[:count].reshape(norms.shape), flat[count:].reshape(biases.shape))


    def send_heads(self, qkv, out):
        size = out.shape[1] // self.ctx_count
        parts = []
        for step in range(self.ctx_count):
            start = (self.ctx ^ step) * size
            piece = jnp.concatenate(
                [
                    pair_columns(lax.dynamic_slice_in_dim(qkv, start, size, 2)),
                    lax.dynamic_slice_in_dim(out, start, size, 1),
                ],
                axis=1,
            )
            piece = jnp.moveaxis(piece.reshape(LANES, -1, LANES), 1, 0).reshape(-1, LANES)
            parts.append(self.across(piece, step) if step else piece)
        return parts

    def cut_layer(self, heads, gate_up, down):
        arrays = [jnp.moveaxis(gate_up, 1, 0), down]
        rows = 3 * down.shape[1] // self.ctx_count
        if heads is not None:
            qkv, out = heads
            arrays = [jnp.moveaxis(qkv, 1, 0), out] + arrays
            rows += 4 * out.shape[1] // self.ctx_count
        return local_kernel(
            functools.partial(cut_kernel, self.ctx_count, heads is not None),
            self.ctx,
            arrays,
            jax.ShapeDtypeStruct((self.ctx_count, rows, LANES), low),
        )

    def send_cut(self, cut):
        return [self.across(cut[k], k) if k else cut[k] for k in range(self.ctx_count)]

    def join_parts(self, parts, units, columns):
        features = LANES * self.ctx_count
        return local_kernel(
            functools.partial(join_kernel, self.ctx_count, len(units)),
            self.ctx,
            parts,
            [jax.ShapeDtypeStruct((size, features), low) for size in units]
            + [jax.ShapeDtypeStruct((features, size), low) for size in columns],
        )

    def split_send(self, value):
        if not self.paired:
            return [value]
        parts = []
        for step in range(self.ctx_count):
            piece = lax.dynamic_slice_in_dim(value, (self.ctx ^ step) * LANES, LANES, 1)
            parts.append(self.across(piece, step) if step else piece)
        return parts

    def join_units(self, parts, tp_units, layer, layer_total, earlier):
        units = tp_units // self.ctx_count
        if not self.paired:
            gate_up = parts[0][: 2 * units].reshape(2, units, -1)
            gate_up = self.spread(gate_up, 2, 1)
            down = self.spread(parts[0][2 * units : 3 * units], 1, 0)
            values = (jnp.transpose(gate_up, (2, 0, 1)), jnp.transpose(down))
            return self.stack_layer(values, layer, layer_total, earlier)
        return stacked_kernel(
            functools.partial(join_units_kernel, self.ctx_count),
            self.ctx,
            parts,
            layer,
            layer_total,
            [(LANES, 2, tp_units), (LANES, tp_units)],
            earlier,
            [pltpu.VMEM((tp_units, LANES), low)],
        )

    def join_heads(self, parts, width, layer, layer_total, earlier):
        if not self.paired:
            columns = 4 * (-(-width // LANES) * LANES)
            qkv = unpair_columns(parts[0][-columns : -columns // 4].T, width)
            out = parts[0][-columns // 4 :].T[:, :width]
            values = (jnp.swapaxes(self.spread(qkv, 0, 2), 0, 1), self.spread(out, 0, 1))
            return self.stack_layer(values, layer, layer_total, earlier)
        tp_width = width * self.ctx_count
        return stacked_kernel(
            functools.partial(join_heads_kernel, self.ctx_count),
            self.ctx,
            parts,
            layer,
            layer_total,
            [(3, LANES, tp_width), (LANES, tp_width)],
            earlier,
        )


    def stack_layer(self, values, layer, layer_total, earlier):
        if earlier is None:
            earlier = [jnp.zeros((layer_total,) + value.shape, full) for value in values]
        return [stack.at[layer].set(value.astype(full)) for stack, value in zip(earlier, values)]

    def spread(self, value, split_axis, join_axis):
        return lax.all_to_all(value, "ctx", split_axis, join_axis, tiled=True)

    def spread_layer(self, qkv, out, gate_up, down):
        gate_up = self.spread(jnp.transpose(gate_up, (1, 2, 0)), 1, 2)
        return (
            over_shard(pair_columns(self.spread(qkv, 2, 0)), 0),
            over_shard(pad_columns(self.spread(out, 1, 0)), 0),
            over_shard(gate_up.reshape(-1, gate_up.shape[2]), 1),
            over_shard(self.spread(jnp.transpose(down), 0, 1), 1),
        )


def pair_columns(weight):
    width = weight.shape[-1]
    pairs = -(-width // LANES)
    if pairs * LANES != width:
        weight = jnp.pad(weight, [(0, 0)] * (weight.ndim - 1) + [(0, pairs * LANES - width)])
    lead = weight.shape[:-2]
    weight = weight.reshape(lead + (3, pairs, LANES))
    return jnp.moveaxis(weight, -2, -3).reshape(lead + (pairs * 3 * LANES,))


def unpair_columns(value, width):
    lead = value.shape[:-1]
    pairs = value.shape[-1] // (3 * LANES)
    value = jnp.moveaxis(value.reshape(lead + (pairs, 3, LANES)), -3, -2)
    return value.reshape(lead + (3, pairs * LANES))[..., :width]


def pad_columns(weight):
    width = weight.shape[-1]
    filled = -(-width // LANES) * LANES
    return weight if filled == width else jnp.pad(weight, [(0, 0), (0, filled - width)])


def sum_dots(groups):
    return jnp.concatenate([dot_tn(lefts[0], rights[0]) for lefts, rights in groups]).astype(low)


def flat_pieces(slots_done):
    return [[piece for pieces in kind for piece in pieces] for kind in zip(*slots_done)]


def over_shard(value, axis):
    return lax.all_gather(value, "shard", axis=axis, tiled=True)


def sum_shard(value, axis):
    return lax.psum_scatter(value, "shard", scatter_dimension=axis, tiled=True)


def body(
    tokens,
    cotangent,
    lengths,
    norm_gain,
    norm_bias,
    input_bias,
    input_projection,
    output_projection,
    gate_up_weight,
    down_weight,
):
    held_rows = tokens.shape[0]
    layer_total = input_projection.shape[0]
    tp_width = input_bias.shape[2]
    ctx_count, tp_count = lax.axis_size("ctx"), lax.axis_size("tp")
    width = tp_width // ctx_count
    hidden_width = down_weight.shape[2] // ctx_count
    rows = held_rows // tp_count
    group = Group(width, hidden_width, input_projection.shape[1], rows)
    seq_ids, length, offset = row_meta(lengths[0], held_rows)
    positions = (
        jnp.arange(ctx_count, dtype=jnp.int32)[:, None] * length[None, :] + offset[None, :]
    ).reshape(-1)
    lane = jnp.arange(LANES, dtype=jnp.int32)[None, :]
    same = lane == seq_ids[:, None]
    named = lane < lengths.shape[1]
    query_mark = jnp.where(named & ~same, blocked, 0.0).astype(low)
    key_mark = jnp.where(same, 1.0, 0.0).astype(low)
    tables = wide_rotary_tables(positions) + (query_mark, key_mark)
    order = group.order()
    bias_own = lax.dynamic_slice_in_dim(input_bias, group.ctx * width, width, 2)
    bias_pairs = pair_columns(bias_own).reshape(layer_total, -1, 3, LANES)

    def own_rows(value):
        return lax.dynamic_slice_in_dim(value, group.tp * rows, rows, 0)

    def sources(index):
        return (
            input_projection[index],
            output_projection[index],
            gate_up_weight[index],
            down_weight[index],
        )

    def norm_one(index, stream):
        scaled, inverse, normed = norm_parts(stream, norm_gain[index, 0], norm_bias[index, 0])
        return (scaled, inverse, group.send_rows(normed.astype(low)))

    stream = own_rows(tokens).astype(full)
    qkv_columns = 3 * width

    def split_heads(heads_full):
        return (heads_full, heads_full[:, qkv_columns:])

    def split_units(units_full):
        return (
            units_full[:hidden_width],
            units_full[hidden_width : 2 * hidden_width],
            units_full[2 * hidden_width :],
        )

    if group.paired:
        (heads_part,) = group.join_parts(
            group.send_heads(*sources(0)[:2]), [], [qkv_columns + width]
        )
        heads_full = over_shard(heads_part, 0)
        first_norm = norm_one(0, stream)
        cut = tied(group.cut_layer(None, *sources(0)[2:]), first_norm[2])[0]
        (units_part,) = group.join_parts(group.send_cut(cut), [3 * hidden_width], [])
        weights = [split_heads(heads_full) + (over_shard(units_part, 1),)]
    else:
        first_norm = norm_one(0, stream)
        weights = []
        for index in range(layer_total):
            qkv_full, out_full, gate_up_full, down_full = group.spread_layer(*sources(index))
            weights.append(
                (qkv_full, out_full)
                + (jnp.concatenate([gate_up_full, down_full], axis=0),)
            )

    saved = []
    for index in range(layer_total):
        last = index + 1 == layer_total
        qkv_weight, out_weight, units_full = weights[index]
        gate_weight, up_weight, down = split_units(units_full)
        scaled_one, inverse_one, arrived = norm_one(index, stream) if index else first_norm
        normed_one = group.receive_pieces(arrived)
        travel = None
        if last:
            grad_own, normed_one = tied(own_rows(cotangent), normed_one)
            travel = group.send_direct(grad_own)
        elif group.paired:
            travel = group.send_cut(
                tied(
                    group.cut_layer(sources(index + 1)[:2], *sources(index + 1)[2:]), normed_one
                )[0]
            )
        heads, fine, totals, rotated = attend(
            order, normed_one, qkv_weight, bias_pairs[index], tables, ctx_count, tp_count
        )
        if travel is not None:
            heads, travel = tied(heads, travel)
        if group.paired and not last:
            units_part, heads_part = group.join_parts(
                travel, [3 * hidden_width], [qkv_columns + width]
            )
            heads = tied(heads, (units_part, heads_part))[0]
            weights.append(
                split_heads(over_shard(heads_part, 0)) + (over_shard(units_part, 1),)
            )
        attention = group.reduce_rows(
            group.chip_sums([dot_nt(rows_in, out_weight) for rows_in in heads])
        )
        middle = stream + attention
        if last:
            (last_branch, units_full), middle = tied(
                (group.direct_pieces(travel), units_full), middle
            )
            gate_weight, up_weight, down = split_units(units_full)
            weights[index] = (qkv_weight, out_weight, units_full)
        scaled_two, inverse_two, normed_two = norm_parts(
            middle, norm_gain[index, 1], norm_bias[index, 1]
        )

        def forward_units(pieces, slot):
            if group.paired and not last:
                feeds, gates, ups, hidden = units_call(pieces, units_full)
                return ((pieces, gates, ups, hidden, feeds), feeds)
            gates = [dot_nt(rows_in, gate_weight) for rows_in in pieces]
            ups = [dot_nt(rows_in, up_weight) for rows_in in pieces]
            hidden = [(jax.nn.silu(gate) * up).astype(low) for gate, up in zip(gates, ups)]
            feeds = [dot_nn(units, down) for units in hidden if not last]
            return ((pieces, gates, ups, hidden, feeds), hidden)

        arrived = group.send_rows(normed_two.astype(low))
        if last:
            slots_done = group.receive_rows(arrived, forward_units)
            normed_two, gates, ups, hidden, feeds = flat_pieces(slots_done)
        else:
            pieces = lax.optimization_barrier(group.receive_pieces(arrived))
            size = len(pieces) // (4 if group.paired else 1)
            slots_done = [
                forward_units(pieces[i : i + size], i // size)[0]
                for i in range(0, len(pieces), size)
            ]
            normed_two, gates, ups, hidden, feeds = flat_pieces(slots_done)
            feeds = group.chip_sums(feeds)
            stream = middle + group.reduce_rows(feeds)
            if group.paired:
                stream, heads_full = tied(stream, weights[index + 1][0])
                weights[index + 1] = split_heads(heads_full) + weights[index + 1][2:]
        saved.append(
            (
                scaled_one,
                inverse_one,
                normed_one,
                heads,
                fine,
                totals,
                rotated,
                scaled_two,
                inverse_two,
                normed_two,
                gates,
                ups,
                hidden,
            )
        )

    grad_stream = own_rows(cotangent).astype(full)
    norm_list = [None] * layer_total
    input_bias_list = [None] * layer_total
    head_stacks = None
    unit_stacks = None
    waiting = None
    for index in reversed(range(layer_total)):
        last = index + 1 == layer_total
        (
            scaled_one,
            inverse_one,
            normed_one,
            heads,
            fine,
            totals,
            rotated,
            scaled_two,
            inverse_two,
            normed_two,
            gates,
            ups,
            hidden,
        ) = saved[index]
        qkv_weight, out_weight, units_full = weights[index]
        gate_weight, up_weight, down = split_units(units_full)


        def backward_units(pieces, slot):
            grad_gates, grad_ups, partials = [], [], []
            for place, rows_in in enumerate(pieces, slot * len(pieces)):
                gate, up = gates[place].astype(full), ups[place].astype(full)
                grad_hidden = dot_nt(rows_in, down)
                sigmoid_gate = jax.nn.sigmoid(gate)
                grad_gates.append(
                    (
                        grad_hidden * up * (sigmoid_gate * (1.0 + gate * (1.0 - sigmoid_gate)))
                    ).astype(low)
                )
                grad_ups.append((grad_hidden * (gate * sigmoid_gate)).astype(low))
                partials.append(
                    dot_nn(grad_gates[-1], gate_weight) + dot_nn(grad_ups[-1], up_weight)
                )
            return ((pieces, grad_gates, grad_ups, partials), (grad_gates, grad_ups))

        if last:
            size = len(last_branch) // (4 if group.paired else 1)
            slots_done = [
                backward_units(last_branch[i : i + size], i // size)[0]
                for i in range(0, len(last_branch), size)
            ]
        else:
            slots_done = group.receive_rows(
                group.send_rows(grad_stream.astype(low)), backward_units
            )
        branch, grad_gates, grad_ups, partials = flat_pieces(slots_done)
        sums = group.chip_sums(partials)
        (branch, grad_gates, grad_ups, hidden), unused = tied(
            (branch, grad_gates, grad_ups, hidden), sums
        )
        if group.paired:
            down_grad = weight_grads([(hidden, branch)], 3 * hidden_width, 2 * hidden_width)
            grad_normed_two, units_grad = group.reduce_rows(
                sums,
                down_grad,
                lambda earlier: weight_grads(
                    [(grad_gates, normed_two), (grad_ups, normed_two)],
                    3 * hidden_width,
                    0,
                    earlier,
                ),
            )
        else:
            units_grad = sum_dots(
                [(grad_gates, normed_two), (grad_ups, normed_two), (hidden, branch)]
            )
            grad_normed_two = group.reduce_rows(sums)
        units_part = sum_shard(units_grad, 1)
        if last:
            feeds = group.chip_sums([dot_nn(units, down) for units in hidden])
        grad_input_two, gain_two, bias_two = norm_back(
            grad_normed_two, scaled_two, inverse_two, norm_gain[index, 1]
        )
        grad_middle = grad_stream + grad_input_two
        branch = group.receive_pieces(group.send_rows(grad_middle.astype(low)))
        grad_heads = [dot_nn(rows_in, out_weight).astype(low) for rows_in in branch]
        if last:
            travel = group.send_sums(tied(feeds, grad_heads)[0])
        else:
            travel = group.split_send(tied(waiting, grad_heads)[0])
        grad_qkv, bias_sums = attend_back(
            order, rotated, grad_heads, fine, totals, tables, ctx_count, tp_count
        )
        grad_qkv, travel, branch = lax.optimization_barrier((grad_qkv, travel, branch))
        if last:
            result = group.both_halves((middle + group.add_sums(travel)).astype(low))
        else:
            unit_stacks = group.join_units(
                travel, hidden_width * ctx_count, index + 1, layer_total, unit_stacks
            )
            head_stacks = group.join_heads(travel, width, index + 1, layer_total, head_stacks)
        sums = group.chip_sums(
            [dot_nt(rows_in, qkv_weight[:, : rows_in.shape[1]]) for rows_in in grad_qkv]
        )
        if group.paired:
            grad_normed_one, heads_grad = group.reduce_rows(
                sums,
                (grad_qkv, branch),
                lambda held: weight_grads([(held[0], normed_one), (heads, held[1])]),
                index == 0,
            )
        else:
            heads_grad = sum_dots([(grad_qkv, normed_one), (heads, branch)])
            grad_normed_one = group.reduce_rows(sums)
        grad_normed_one, (units_part, result) = tied(grad_normed_one, (units_part, result))
        heads_part = sum_shard(heads_grad, 1)
        if index:
            waiting = jnp.concatenate([units_part, heads_part], axis=0)
        bias_sums = bias_sums[:, :3, :].transpose(1, 0, 2).reshape(3, -1)[:, :width]
        input_bias_list[index] = lax.dynamic_update_slice_in_dim(
            jnp.zeros((3, tp_width), full), bias_sums, group.ctx * width, 1
        )
        grad_input_one, gain_one, bias_one = norm_back(
            grad_normed_one, scaled_one, inverse_one, norm_gain[index, 0]
        )
        grad_stream = grad_middle + grad_input_one
        norm_list[index] = jnp.stack([gain_one, gain_two, bias_one, bias_two])
    unit_stacks = group.join_units(
        group.split_send(units_part), hidden_width * ctx_count, 0, layer_total, unit_stacks
    )
    norm_total, bias_total = group.total(jnp.stack(norm_list), jnp.stack(input_bias_list))
    tokens_grad = group.both_halves(grad_stream)
    heads_part = tied(heads_part, (unit_stacks, norm_total, bias_total, result, tokens_grad))[0]
    head_stacks = group.join_heads(
        group.split_send(heads_part), width, 0, layer_total, head_stacks
    )
    return (
        result,
        tokens_grad,
        norm_total[:, :2],
        norm_total[:, 2:],
        bias_total,
        jnp.moveaxis(head_stacks[0], 1, 2),
        head_stacks[1],
        unit_stacks[0],
        unit_stacks[1],
    )


def solution(mesh):
    in_specs = (
        P(("shard", "ctx"), None),
        P(("shard", "ctx"), None),
        P("shard", None),
        P(),
        P(),
        P(None, None, "tp"),
        P(None, ("shard", "ctx"), None, "tp"),
        P(None, ("shard", "ctx"), "tp"),
        P(None, ("shard", "ctx"), None, "tp"),
        P(None, ("shard", "ctx"), "tp"),
    )
    out_specs = (
        P(("shard", "ctx"), None),
        P(("shard", "ctx"), None),
        P(),
        P(),
        P(None, None, "tp"),
        P(None, ("shard", "ctx"), None, "tp"),
        P(None, ("shard", "ctx"), "tp"),
        P(None, ("shard", "ctx"), None, "tp"),
        P(None, ("shard", "ctx"), "tp"),
    )
    return jax.shard_map(body, mesh=mesh, in_specs=in_specs, out_specs=out_specs, check_vma=False)
```
